128 devices in a mesh: gx: 8 (over z, y_hi), gy: 4 (over x), gz: 4 (over y_lo, core).
Axes of the slice: x: 4, y: 4 (y_hi: 2, y_lo: 2; y = y_hi * 2 + y_lo), z: 4, core: 2. Of those that a mesh axis runs over, the one named last changes fastest.
Arguments:
- normed: bfloat16 [2560, 6144], P(('gx', 'gy'), 'gz'), may hold values from -6 to 6
- context: bfloat16 [2560, 6144], P('gz', ('gx', 'gy')), may hold values from -6 to 6
- hidden_pre: bfloat16 [2560, 24576], P('gz', ('gx', 'gy')), may hold values from -6 to 6
- grad_out: bfloat16 [2560, 6144], P(('gx', 'gy'), 'gz'), may hold values from -6 to 6
- w_in: bfloat16 [6144, 24576], P('gz', ('gx', 'gy')), may hold values from -0.078125 to 0.078125
- w_out: bfloat16 [24576, 6144], P(('gx', 'gy'), 'gz'), may hold values from -0.0390625 to 0.0390625
- w_proj: bfloat16 [6144, 6144], P(('gx', 'gy'), 'gz'), may hold values from -0.078125 to 0.078125
Outputs:
- grad_normed: bfloat16 [2560, 6144], P(('gx', 'gy'), 'gz')
- grad_context: bfloat16 [2560, 6144], P('gz', ('gx', 'gy'))
- grad_w_in: bfloat16 [6144, 24576], P('gz', ('gx', 'gy'))
- grad_w_out: bfloat16 [24576, 6144], P(('gx', 'gy'), 'gz')
- grad_w_proj: bfloat16 [6144, 6144], P(('gx', 'gy'), 'gz')
The draws below stay inside these ranges and needn't reach their ends.
All inputs are finite; a program needn't handle non-finite values.
Results may differ from the reference program's by a relative error of at most 0.0051.
Values may be sent and summed in bfloat16 or wider, within the bound.
A program may use at most 128 MiB of HBM per device.

```python
import math
import jax
import jax.numpy as jnp
from jax import lax

D = 6144
FF = 24576
TOKENS = 2560


def level_of(rng, shape, pieces, low, high):
    def one(position, blocks):
        heights = jax.random.uniform(jax.random.fold_in(jax.random.fold_in(rng, 6), position), (blocks,), jnp.float32, low / len(pieces), high / len(pieces))
        return jnp.repeat(jnp.exp(heights), shape[position] // blocks).reshape((-1,) + (1,) * (len(shape) - position - 1))

    level = one(*pieces[0])
    for cut in pieces[1:]:
        level = level * one(*cut)
    return level


def centred(own_key, shape, deviation, limit, split=(), held_as=jnp.bfloat16):
    result = deviation * jax.random.normal(own_key, shape, jnp.float32)
    if split:
        result = result * level_of(own_key, shape, split, -0.22, 0.18)
    return jnp.clip(result, -limit, limit).astype(held_as)


def setup_inputs(seed: int = 0) -> dict:
    arg_keys = jax.random.split(jax.random.key(seed), 8)
    return {
        "normed": centred(arg_keys[0], (TOKENS, D), 1.0, 6.0, ((0, 32), (1, 4))),
        "context": centred(arg_keys[1], (TOKENS, D), 1.0, 6.0, ((0, 4), (1, 32))),
        "hidden_pre": centred(arg_keys[2], (TOKENS, FF), 1.0, 6.0, ((0, 4), (1, 32))),
        "grad_out": centred(arg_keys[3], (TOKENS, D), 1.0, 6.0, ((0, 32), (1, 4))),
        "w_in": centred(arg_keys[4], (D, FF), D ** -0.5, 0.078125, ((0, 4), (1, 32))),
        "w_out": centred(arg_keys[5], (FF, D), FF ** -0.5, 0.0390625, ((0, 32), (1, 4))),
        "w_proj": centred(arg_keys[6], (D, D), D ** -0.5, 0.078125, ((0, 32), (1, 4))),
    }


inv_root_two = 0.7071067811865476
inv_root_two_pi = 0.3989422804014327

def gelu_parts(hidden_pre):
    values = hidden_pre.astype(jnp.float32)
    normal_cdf = 0.5 * (1.0 + jax.scipy.special.erf(values * inv_root_two))
    density = jnp.exp(-0.5 * values * values) * inv_root_two_pi
    return (values * normal_cdf, normal_cdf + values * density)

def contract_rows(left, right):
    return lax.dot_general(left, right, (((0,), (0,)), ((), ())), preferred_element_type=jnp.float32)

def contract_cols(left, right):
    return lax.dot_general(left, right, (((1,), (1,)), ((), ())), preferred_element_type=jnp.float32)

def reference(normed, context, hidden_pre, grad_out, w_in, w_out, w_proj):
    grad_scale = 1.0 / math.sqrt(TOKENS)
    grad_act = contract_cols(grad_out, w_out)
    activated_f, gelu_slope = gelu_parts(hidden_pre)
    activated = activated_f.astype(jnp.bfloat16)
    grad_hidden = (grad_act * gelu_slope).astype(jnp.bfloat16)
    grad_w_out = (contract_rows(activated, grad_out) * grad_scale).astype(jnp.bfloat16)
    grad_w_in = (contract_rows(normed, grad_hidden) * grad_scale).astype(jnp.bfloat16)
    grad_normed = contract_cols(grad_hidden, w_in).astype(jnp.bfloat16)
    grad_w_proj = (contract_rows(context, grad_out) * grad_scale).astype(jnp.bfloat16)
    grad_context = contract_cols(grad_out, w_proj).astype(jnp.bfloat16)
    return (grad_normed, grad_context, grad_w_in, grad_w_out, grad_w_proj)
```

```python
import math

import jax
import jax.numpy as jnp
from jax import lax
from jax.experimental import pallas as pl
from jax.experimental.pallas import tpu as pltpu
from jax.sharding import PartitionSpec as P

MESH = pl.DeviceIdType.MESH
inv_root_two = 0.7071067811865476
inv_root_two_pi = 0.3989422804014327


def gelu_parts(hidden_pre):
    values = hidden_pre.astype(jnp.float32)
    normal_cdf = 0.5 * (1.0 + jax.scipy.special.erf(values * inv_root_two))
    density = jnp.exp(-0.5 * values * values) * inv_root_two_pi
    return (values * normal_cdf, normal_cdf + values * density)


def contract_rows(left, right):
    return lax.dot_general(
        left, right, (((0,), (0,)), ((), ())), preferred_element_type=jnp.float32
    )


def contract_cols(left, right):
    return lax.dot_general(
        left, right, (((1,), (1,)), ((), ())), preferred_element_type=jnp.float32
    )


class Place:
    def __init__(self):
        gx, gy, gz = (lax.axis_index(a) for a in ("gx", "gy", "gz"))
        self.z, self.yh, self.x = gx // 2, lax.rem(gx, 2), gy
        z, yh, x = self.z, self.yh, self.x
        zp, zm, z2 = (lax.rem(z + k, 4) for k in (1, 3, 2))
        xp, xm, x2 = (lax.rem(x + k, 4) for k in (1, 3, 2))
        self.zs = (z, zp, zm, z2)
        self.xs = (x, xp, xm, x2)
        self.dev = {
            "x+": (gx, xp, gz),
            "x-": (gx, xm, gz),
            "z+": (zp * 2 + yh, x, gz),
            "z-": (zm * 2 + yh, x, gz),
            "yh": (z * 2 + 1 - yh, x, gz),
        }


class Links:
    def __init__(self, place, send_sems, recv_sems):
        self.place, self.ss, self.rs = place, send_sems, recv_sems
        self.names, self.started = {}, []

    def copy(self, key, src, dst, to):
        i = self.names.setdefault(key, len(self.names))
        return pltpu.make_async_remote_copy(
            src_ref=src, dst_ref=dst, send_sem=self.ss.at[i], recv_sem=self.rs.at[i],
            device_id=self.place.dev[to], device_id_type=MESH)

    def send(self, key, src, dst, to):
        c = self.copy(key, src, dst, to)
        c.start()
        self.started.append(c)

    def got(self, key, view):
        self.copy(key, view, view, "x+").wait_recv()


class Gather:
    def __init__(self, name, full, place, links):
        self.name, self.full, self.p, self.l = name, full, place, links
        self.first = (("x+", "x-"), ("z+", "z-"))
        self.second = (("z+", "z-"), ("x+", "x-"))
        self.one = (place.xs, place.zs)
        self.two = (place.zs, place.xs)

    def view(self, part, yy, i, j, half=None):
        zz, xx = (j, i) if part == 0 else (i, j)
        width = self.full.shape[-1] // 2
        start, n = part * width, width
        if half is not None:
            n = width // 2
            start += half * n
        return self.full.at[zz, yy, xx, :, pl.ds(start, n)]

    def send(self, key, view, to):
        self.l.send((self.name,) + key, view, view, to)

    def got(self, key, view):
        self.l.got((self.name,) + key, view)

    def exchange(self):
        own = self.full.at[self.p.z, self.p.yh, self.p.x]
        self.send(("y",), own, "yh")

    def exchanged(self):
        self.got(("y",), self.full.at[self.p.z, self.p.yh, self.p.x])

    def r0(self, w, yy):
        for key, ways in (("f", self.first), ("s0", self.second)):
            for p in (0, 1):
                own = self.view(p, yy, self.one[p][0], self.two[p][0])
                for s in (0, 1):
                    self.send((w, p, key, s), own, ways[p][s])

    def r1(self, w, yy):
        for p in (0, 1):
            i0, ip, im, i2 = self.one[p]
            j0 = self.two[p][0]
            self.got((w, p, "f", 0), self.view(p, yy, im, j0))
            self.send((w, p, "ff", 0), self.view(p, yy, im, j0, 0), self.first[p][0])
            self.got((w, p, "f", 1), self.view(p, yy, ip, j0))
            self.send((w, p, "ff", 1), self.view(p, yy, ip, j0, 1), self.first[p][1])
        for p in (0, 1):
            i0, ip, im, i2 = self.one[p]
            j0 = self.two[p][0]
            for k, i in (("s1", im), ("s2", ip)):
                for s in (0, 1):
                    self.send((w, p, k, s), self.view(p, yy, i, j0), self.second[p][s])

    def r2(self, w, yy):
        for p in (0, 1):
            i2, j0 = self.one[p][3], self.two[p][0]
            for h in (0, 1):
                self.got((w, p, "ff", h), self.view(p, yy, i2, j0, h))
            for s in (0, 1):
                self.send((w, p, "s3", s), self.view(p, yy, i2, j0), self.second[p][s])

    def order(self, p, k):
        i0, ip, im, i2 = self.one[p]
        return (i0, im, ip, i2)[k]

    def r3(self, w, yy, k):
        for p in (0, 1):
            i = self.order(p, k)
            j0, jp, jm, j2 = self.two[p]
            self.got((w, p, f"s{k}", 0), self.view(p, yy, i, jm))
            self.send((w, p, f"sf{k}", 0), self.view(p, yy, i, jm, 0), self.second[p][0])
            self.got((w, p, f"s{k}", 1), self.view(p, yy, i, jp))
            self.send((w, p, f"sf{k}", 1), self.view(p, yy, i, jp, 1), self.second[p][1])

    def r4(self, w, yy, k):
        for p in (0, 1):
            i, j2 = self.order(p, k), self.two[p][3]
            for h in (0, 1):
                self.got((w, p, f"sf{k}", h), self.view(p, yy, i, j2, h))


SEMS = 192


def gather_kernel(g_ref, n_ref, g_full, n_full, ss, rs, lsem):
    place = Place()
    z, yh, x = place.z, place.yh, place.x
    bar = pltpu.get_barrier_semaphore()
    for d in place.dev.values():
        pl.semaphore_signal(bar, inc=1, device_id=d, device_id_type=MESH)
    local = [
        pltpu.make_async_copy(g_ref, g_full.at[z, yh, x], lsem.at[0]),
        pltpu.make_async_copy(n_ref, n_full.at[z, yh, x], lsem.at[1]),
    ]
    for c in local:
        c.start()
    pl.semaphore_wait(bar, len(place.dev))
    for c in local:
        c.wait()
    links = Links(place, ss, rs)
    a, b = Gather("g", g_full, place, links), Gather("n", n_full, place, links)
    o = 1 - yh
    a.exchange()
    b.exchange()
    a.r0(0, yh)
    a.r1(0, yh)
    a.r3(0, yh, 0)
    a.r2(0, yh)
    a.exchanged()
    waves = [(a, 0, yh), (a, 1, o), (b, 0, yh), (b, 1, o)]
    for k, (u, w, yy) in enumerate(waves):
        after = waves[k + 1] if k + 1 < len(waves) else None
        if after:
            v, w2, y2 = after
            if k == 2:
                b.exchanged()
            v.r0(w2, y2)
        u.r3(w, yy, 1)
        u.r3(w, yy, 2)
        if after:
            v.r1(w2, y2)
        u.r3(w, yy, 3)
        if after:
            v.r3(w2, y2, 0)
            v.r2(w2, y2)
        for j in range(4):
            u.r4(w, yy, j)
    for c in links.started:
        c.wait_send()


def gather_both(grad_out, normed):
    shape = jax.ShapeDtypeStruct((4, 2, 4) + grad_out.shape, grad_out.dtype)
    g, n = pl.pallas_call(
        gather_kernel,
        out_shape=[shape, shape],
        in_specs=[pl.BlockSpec(memory_space=pl.ANY)] * 2,
        out_specs=[pl.BlockSpec(memory_space=pl.ANY)] * 2,
        scratch_shapes=[
            pltpu.SemaphoreType.DMA((SEMS,)),
            pltpu.SemaphoreType.DMA((SEMS,)),
            pltpu.SemaphoreType.DMA((2,)),
        ],
        compiler_params=pltpu.CompilerParams(collective_id=0, has_side_effects=True),
    )(grad_out, normed)
    rows = 32 * grad_out.shape[0]
    return g.reshape(rows, grad_out.shape[1]), n.reshape(rows, grad_out.shape[1])


def body(normed, context, hidden_pre, grad_out, w_in, w_out, w_proj):
    grad_full, normed_full = gather_both(grad_out, normed)
    hidden_full, context_full = (
        lax.all_gather(hidden_pre, "gz", axis=0, tiled=True),
        lax.all_gather(context, "gz", axis=0, tiled=True),
    )
    grad_scale = 1.0 / math.sqrt(grad_full.shape[0])
    activated_f, slope_full = gelu_parts(hidden_full)
    activated = activated_f.astype(jnp.bfloat16)
    panel = grad_full
    grad_share = lax.psum_scatter(
        contract_cols(panel, w_out), "gz", scatter_dimension=0, tiled=True
    )
    local_act, local_slope = gelu_parts(hidden_pre)
    hidden_share = (grad_share * local_slope).astype(jnp.bfloat16)
    grad_hidden = lax.all_gather(hidden_share, "gz", axis=0, tiled=True)
    grad_w_out = (contract_rows(activated, grad_full) * grad_scale).astype(jnp.bfloat16)
    grad_w_in = (contract_rows(normed_full, grad_hidden) * grad_scale).astype(jnp.bfloat16)
    grad_w_proj = (contract_rows(context_full, grad_full) * grad_scale).astype(jnp.bfloat16)
    panel = grad_hidden
    grad_normed = lax.psum_scatter(
        contract_cols(panel, w_in), ("gx", "gy"), scatter_dimension=0, tiled=True
    ).astype(jnp.bfloat16)
    panel = grad_full
    grad_context = lax.psum_scatter(
        contract_cols(panel, w_proj), "gz", scatter_dimension=0, tiled=True
    ).astype(jnp.bfloat16)
    return (grad_normed, grad_context, grad_w_in, grad_w_out, grad_w_proj)


def solution(mesh):
    in_specs = (
        P(("gx", "gy"), "gz"),
        P("gz", ("gx", "gy")),
        P("gz", ("gx", "gy")),
        P(("gx", "gy"), "gz"),
        P("gz", ("gx", "gy")),
        P(("gx", "gy"), "gz"),
        P(("gx", "gy"), "gz"),
    )
    out_specs = (
        P(("gx", "gy"), "gz"),
        P("gz", ("gx", "gy")),
        P("gz", ("gx", "gy")),
        P(("gx", "gy"), "gz"),
        P(("gx", "gy"), "gz"),
    )
    return jax.shard_map(body, mesh=mesh, in_specs=in_specs, out_specs=out_specs, check_vma=False)
```

```python
import math

import jax
import jax.numpy as jnp
from jax import lax
from jax.experimental import pallas as pl
from jax.experimental.pallas import tpu as pltpu
from jax.sharding import PartitionSpec as P

MESH = pl.DeviceIdType.MESH
f32, bf16 = jnp.float32, jnp.bfloat16
inv_root_two = 0.7071067811865476
inv_root_two_pi = 0.3989422804014327
SEMS = 320


def nt(left, right):
    return lax.dot_general(left, right, (((1,), (1,)), ((), ())), preferred_element_type=f32)


def tn(left, right):
    return lax.dot_general(left, right, (((0,), (0,)), ((), ())), preferred_element_type=f32)


class Place:
    def __init__(self, block):
        gx, gy, gz = (lax.axis_index(a) for a in ("gx", "gy", "gz"))
        self.block = block
        self.z, self.yh, self.x, self.gz = gx // 2, lax.rem(gx, 2), gy, gz
        self.yl, self.c = gz // 2, lax.rem(gz, 2)
        z, yh, x = self.z, self.yh, self.x
        zp, zm, z2 = (lax.rem(z + k, 4) for k in (1, 3, 2))
        xp, xm, x2 = (lax.rem(x + k, 4) for k in (1, 3, 2))
        self.zs = (z, zp, zm, z2)
        self.xs = (x, xp, xm, x2)
        self.dev = {
            "x+": (gx, xp, gz),
            "x-": (gx, xm, gz),
            "z+": (zp * 2 + yh, x, gz),
            "z-": (zm * 2 + yh, x, gz),
            "yh": (z * 2 + 1 - yh, x, gz),
            "yl": (gx, gy, (1 - self.yl) * 2 + self.c),
            "c": (gx, gy, self.yl * 2 + 1 - self.c),
        }

    def rows(self, z, yh, x):
        return pl.ds(pl.multiple_of((z * 8 + yh * 4 + x) * self.block, self.block), self.block)

    def chunk(self, z, yh):
        n = 4 * self.block
        return pl.ds(pl.multiple_of((z * 2 + yh) * n, n), n)

    def shard(self, j):
        n = 8 * self.block
        return pl.ds(pl.multiple_of(j * n, n), n)


class Links:
    def __init__(self, place, send_sems, recv_sems):
        self.place, self.ss, self.rs = place, send_sems, recv_sems
        self.names, self.started = {}, []

    def copy(self, key, src, dst, to):
        i = self.names.setdefault(key, len(self.names))
        return pltpu.make_async_remote_copy(
            src_ref=src, dst_ref=dst, send_sem=self.ss.at[i], recv_sem=self.rs.at[i],
            device_id=self.place.dev[to], device_id_type=MESH)

    def send(self, key, src, dst, to):
        c = self.copy(key, src, dst, to)
        c.start()
        self.started.append(c)

    def got(self, key, view):
        self.copy(key, view, view, "x+").wait_recv()

    def sent(self):
        for c in self.started:
            c.wait_send()
        self.started = []


class Gather:
    def __init__(self, name, full, place, links):
        self.name, self.full, self.p, self.l = name, full, place, links
        self.first = (("x+", "x-"), ("z+", "z-"))
        self.second = (("z+", "z-"), ("x+", "x-"))
        self.one = (place.xs, place.zs)
        self.two = (place.zs, place.xs)

    def view(self, part, yy, i, j, half=None):
        zz, xx = (j, i) if part == 0 else (i, j)
        width = self.full.shape[-1] // 2
        start, n = part * width, width
        if half is not None:
            n = width // 2
            start += half * n
        return self.full.at[self.p.rows(zz, yy, xx), pl.ds(start, n)]

    def send(self, key, view, to):
        self.l.send((self.name,) + key, view, view, to)

    def got(self, key, view):
        self.l.got((self.name,) + key, view)

    def exchange(self):
        own = self.full.at[self.p.rows(self.p.z, self.p.yh, self.p.x)]
        self.send(("y",), own, "yh")

    def exchanged(self):
        self.got(("y",), self.full.at[self.p.rows(self.p.z, 1 - self.p.yh, self.p.x)])

    def r0(self, w, yy):
        for key, ways in (("f", self.first), ("s0", self.second)):
            for p in (0, 1):
                own = self.view(p, yy, self.one[p][0], self.two[p][0])
                for s in (0, 1):
                    self.send((w, p, key, s), own, ways[p][s])

    def r1(self, w, yy):
        for p in (0, 1):
            i0, ip, im, i2 = self.one[p]
            j0 = self.two[p][0]
            self.got((w, p, "f", 0), self.view(p, yy, im, j0))
            self.send((w, p, "ff", 0), self.view(p, yy, im, j0, 0), self.first[p][0])
            self.got((w, p, "f", 1), self.view(p, yy, ip, j0))
            self.send((w, p, "ff", 1), self.view(p, yy, ip, j0, 1), self.first[p][1])
        for p in (0, 1):
            i0, ip, im, i2 = self.one[p]
            j0 = self.two[p][0]
            for k, i in (("s1", im), ("s2", ip)):
                for s in (0, 1):
                    self.send((w, p, k, s), self.view(p, yy, i, j0), self.second[p][s])

    def r2(self, w, yy):
        for p in (0, 1):
            i2, j0 = self.one[p][3], self.two[p][0]
            for h in (0, 1):
                self.got((w, p, "ff", h), self.view(p, yy, i2, j0, h))
            for s in (0, 1):
                self.send((w, p, "s3", s), self.view(p, yy, i2, j0), self.second[p][s])

    def order(self, p, k):
        i0, ip, im, i2 = self.one[p]
        return (i0, im, ip, i2)[k]

    def r3(self, w, yy, k):
        for p in (0, 1):
            i = self.order(p, k)
            j0, jp, jm, j2 = self.two[p]
            self.got((w, p, f"s{k}", 0), self.view(p, yy, i, jm))
            self.send((w, p, f"sf{k}", 0), self.view(p, yy, i, jm, 0), self.second[p][0])
            self.got((w, p, f"s{k}", 1), self.view(p, yy, i, jp))
            self.send((w, p, f"sf{k}", 1), self.view(p, yy, i, jp, 1), self.second[p][1])

    def r4(self, w, yy, k):
        for p in (0, 1):
            i, j2 = self.order(p, k), self.two[p][3]
            for h in (0, 1):
                self.got((w, p, f"sf{k}", h), self.view(p, yy, i, j2, h))


class Scatter:
    def __init__(self, part_sums, far1, near1, far2, near2, keep, place, links):
        self.d, self.far1, self.near1, self.far2, self.near2, self.keep = part_sums, far1, near1, far2, near2, keep
        self.p, self.l = place, links
        self.first = (("z+", "z-"), ("x+", "x-"))
        self.second = (("x+", "x-"), ("z+", "z-"))
        self.one = (place.zs, place.xs)
        self.two = (place.xs, place.zs)
        self.width = part_sums.shape[-1] // 2

    def view(self, part, yy, i, j, half=None):
        zz, xx = (i, j) if part == 0 else (j, i)
        start, n = part * self.width, self.width
        if half is not None:
            n = self.width // 2
            start += half * n
        return self.d.at[self.p.rows(zz, yy, xx), pl.ds(start, n)]

    def order(self, p, k):
        j0, jp, jm, j2 = self.two[p]
        return (j2, jp, jm, j0)[k]

    def s1(self, w, yy, p):
        for k in range(4):
            for h in (0, 1):
                self.l.send(("rs", w, p, "far1", k, h), self.view(p, yy, self.one[p][3], self.order(p, k), h),
                            self.far1.at[w, p, k, h], self.first[p][h])

    def fold(self, into, *terms):
        total = into[...].astype(f32)
        for t in terms:
            total = total + t[...].astype(f32)
        into[...] = total.astype(into.dtype)

    def s2(self, w, yy, k):
        for p in (0, 1):
            j = self.order(p, k)
            for h in (0, 1):
                i = self.one[p][1 + h]
                self.l.got(("rs", w, p, "far1", k, h), self.far1.at[w, p, k, h])
                self.fold(self.view(p, yy, i, j, h), self.far1.at[w, p, k, h])
                self.l.send(("rs", w, p, "near1", k, h), self.view(p, yy, i, j), self.near1.at[w, p, k, h], self.first[p][h])

    def s3(self, w, yy, k):
        for p in (0, 1):
            for h in (0, 1):
                self.l.got(("rs", w, p, "near1", k, h), self.near1.at[w, p, k, h])
            mine = self.view(p, yy, self.one[p][0], self.order(p, k))
            if k == 3:
                self.keep[w, p] = (mine[...].astype(f32) + self.near1[w, p, k, 0].astype(f32)
                                   + self.near1[w, p, k, 1].astype(f32))
            else:
                self.fold(mine, self.near1.at[w, p, k, 0], self.near1.at[w, p, k, 1])
            if k == 0:
                for h in (0, 1):
                    self.l.send(("rs", w, p, "far2", h), self.view(p, yy, self.one[p][0], self.order(p, k), h),
                                self.far2.at[w, p, h], self.second[p][h])

    def t2(self, w, yy):
        for p in (0, 1):
            for h in (0, 1):
                into = self.view(p, yy, self.one[p][0], self.two[p][1 + h], h)
                self.l.got(("rs", w, p, "far2", h), self.far2.at[w, p, h])
                self.fold(into, self.far2.at[w, p, h])
                self.l.send(("rs", w, p, "near2", h), self.view(p, yy, self.one[p][0], self.two[p][1 + h]),
                            self.near2.at[w, p, h], self.second[p][h])

    def t3(self, w, p):
        for h in (0, 1):
            self.l.got(("rs", w, p, "near2", h), self.near2.at[w, p, h])
        return self.keep[w, p] + self.near2[w, p, 0].astype(f32) + self.near2[w, p, 1].astype(f32)


def kernel(scale, n_in, c_in, h_in, g_in, wi_in, wo_in, wp_in,
           gn_out, gc_out, gwi_out, gwo_out, gwp_out,
           G, N, ACT, CTX, HP, WIN, WOUT, WPROJ, GH, SLOPE, P1S, P1R, POWN, P2S, P2R,
           C1S, C1R, COWN, C2S, C2R, FAR1, NEAR1, FAR2, NEAR2, KEEP, YS, YR, GN, GC, ss, rs, ls):
    block = g_in.shape[0]
    p = Place(block)
    z, yh, x, gz, yl, c = p.z, p.yh, p.x, p.gz, p.yl, p.c
    o = 1 - yh
    chunk_rows = 4 * block

    bar = pltpu.get_barrier_semaphore()
    for d in p.dev.values():
        pl.semaphore_signal(bar, inc=1, device_id=d, device_id_type=MESH)
    loads = {}
    for i, (name, src, dst) in enumerate((
            ("g", g_in, G.at[p.rows(z, yh, x)]), ("h", h_in, HP), ("c", c_in, CTX.at[p.shard(gz)]),
            ("n", n_in, N.at[p.rows(z, yh, x)]), ("wo", wo_in, WOUT), ("wp", wp_in, WPROJ), ("wi", wi_in, WIN))):
        loads[name] = pltpu.make_async_copy(src, dst, ls.at[i])
        loads[name].start()
    stores = []

    def store(src, dst):
        s = pltpu.make_async_copy(src, dst, ls.at[8 + len(stores)])
        s.start()
        stores.append(s)

    pl.semaphore_wait(bar, len(p.dev))

    gl, nl, yl_links, rl = (Links(p, ss, rs) for _ in range(4))
    for other in (nl, yl_links, rl):
        other.names = gl.names
    a, b = Gather("g", G, p, gl), Gather("n", N, p, nl)
    red = Scatter(G, FAR1, NEAR1, FAR2, NEAR2, KEEP, p, rl)
    wave_yh = (yh, o)

    def spread(name, view):
        yl_links.send((name, "y"), view, view, "yl")
        yl_links.send((name, "c"), view, view, "c")

    def relay(name, view_of):
        v = view_of((1 - yl) * 2 + c)
        yl_links.got((name, "y"), v)
        yl_links.send((name, "cy"), v, v, "c")

    def spread_done(name, view_of):
        yl_links.got((name, "c"), view_of(yl * 2 + 1 - c))
        yl_links.got((name, "cy"), view_of((1 - yl) * 2 + 1 - c))

    act_rows = lambda j: ACT.at[p.shard(j)]
    ctx_rows = lambda j: CTX.at[p.shard(j)]

    def gh_rows(w):
        return lambda j: GH.at[p.chunk(j, wave_yh[w])]

    def act_peer(w):
        for s, yy in enumerate((1 - yl, yl)):
            P1S[w, s] = nt(G[p.chunk(yy * 2 + 1 - c, wave_yh[w]), :], WOUT[...])
            yl_links.send(("p1", w, s), P1S.at[w, s], P1R.at[w, s], "c")

    def act_own(w):
        yl_links.got(("p1", w, 0), P1R.at[w, 0])
        P2S[w] = (nt(G[p.chunk((1 - yl) * 2 + c, wave_yh[w]), :], WOUT[...]) + P1R[w, 0]).astype(bf16)
        yl_links.send(("p2", w), P2S.at[w], P2R.at[w], "yl")
        yl_links.got(("p1", w, 1), P1R.at[w, 1])
        POWN[w] = nt(G[p.chunk(gz, wave_yh[w]), :], WOUT[...]) + P1R[w, 1]

    def hidden(w):
        yl_links.got(("p2", w), P2R.at[w])
        n = chunk_rows
        local = pl.ds(pl.multiple_of(wave_yh[w] * n, n), n)
        GH[p.chunk(gz, wave_yh[w]), :] = ((POWN[w] + P2R[w].astype(f32)) * SLOPE[local, :]).astype(bf16)
        spread(("gh", w), gh_rows(w)(gz))

    def ctx_peer():
        for s, yy in enumerate((1 - yl, yl)):
            C1S[s] = nt(G[p.shard(yy * 2 + 1 - c), :], WPROJ[...])
            yl_links.send(("c1", s), C1S.at[s], C1R.at[s], "c")

    def ctx_own():
        yl_links.got(("c1", 0), C1R.at[0])
        C2S[...] = (nt(G[p.shard((1 - yl) * 2 + c), :], WPROJ[...]) + C1R[0]).astype(bf16)
        yl_links.send(("c2",), C2S, C2R, "yl")
        yl_links.got(("c1", 1), C1R.at[1])
        COWN[...] = nt(G[p.shard(gz), :], WPROJ[...]) + C1R[1]

    def ctx_done():
        yl_links.got(("c2",), C2R)
        GC[...] = (COWN[...] + C2R[...].astype(f32)).astype(bf16)
        store(GC, gc_out)

    def w_out_tiles(f):
        @pl.loop(0, 3)
        def _(i):
            cols = pl.ds(pl.multiple_of(i * 512, 512), 512)
            WOUT[pl.ds(f * 256, 256), cols] = (tn(ACT[:, pl.ds(f * 256, 256)], G[:, cols]) * scale).astype(bf16)

    def w_proj_tiles():
        @pl.loop(0, 3)
        def _(i):
            cols = pl.ds(pl.multiple_of(i * 512, 512), 512)
            WPROJ[:, cols] = (tn(CTX[...], G[:, cols]) * scale).astype(bf16)

    def w_in_tiles(start, count):
        @pl.loop(start, start + count)
        def _(i):
            cols = pl.ds(pl.multiple_of(i * 256, 256), 256)
            WIN2[cols, :] = (tn(N[:, cols], GH[...]) * scale).astype(bf16)

    def partial(yy, zz):
        G[p.chunk(zz, yy), :] = nt(GH[p.chunk(zz, yy), :], WIN[...]).astype(bf16)

    def partials(w, yy):
        z0, zp, zm, z2 = p.zs
        partial(yy, z2)
        red.s1(w, yy, 0)

        @pl.loop(0, 3)
        def _(i):
            partial(yy, lax.rem(z2 + 1 + i, 4))

        red.s1(w, yy, 1)

    WIN2 = WIN

    loads["g"].wait()
    a.exchange()
    a.r0(0, yh)
    loads["c"].wait()
    spread("ctx", ctx_rows(gz))
    loads["h"].wait()

    @pl.loop(0, HP.shape[0] // 16)
    def _(i):
        here = pl.ds(pl.multiple_of(i * 16, 16), 16)
        v = HP[here, :].astype(f32)
        cdf = 0.5 * (1.0 + lax.erf(v * inv_root_two))
        density = jnp.exp(-0.5 * v * v) * inv_root_two_pi
        SLOPE[here, :] = cdf + v * density
        ACT[pl.ds(pl.multiple_of(gz * HP.shape[0] + i * 16, 16), 16), :] = (v * cdf).astype(bf16)

    spread("act", act_rows(gz))
    a.r1(0, yh)
    a.r3(0, yh, 0)
    a.r2(0, yh)
    a.exchanged()
    a.r0(1, o)
    a.r3(0, yh, 1)
    a.r3(0, yh, 2)
    a.r1(1, o)
    a.r3(0, yh, 3)
    a.r3(1, o, 0)
    a.r2(1, o)
    loads["n"].wait()
    b.exchange()
    for j in range(4):
        a.r4(0, yh, j)
    b.r0(0, yh)
    loads["wo"].wait()
    act_peer(0)
    a.r3(1, o, 1)
    act_own(0)
    a.r3(1, o, 2)
    relay("ctx", ctx_rows)
    b.r1(0, yh)
    a.r3(1, o, 3)
    b.r3(0, yh, 0)
    b.r2(0, yh)
    relay("act", act_rows)
    for j in range(4):
        a.r4(1, o, j)
    b.exchanged()
    b.r0(1, o)
    act_peer(1)
    b.r3(0, yh, 1)
    act_own(1)
    hidden(0)
    b.r3(0, yh, 2)
    b.r1(1, o)
    loads["wp"].wait()
    ctx_peer()
    b.r3(0, yh, 3)
    b.r3(1, o, 0)
    b.r2(1, o)
    ctx_own()
    spread_done("act", act_rows)
    w_out_tiles(0)
    for j in range(4):
        b.r4(0, yh, j)
    relay(("gh", 0), gh_rows(0))
    hidden(1)
    b.r3(1, o, 1)
    w_out_tiles(1)
    b.r3(1, o, 2)
    w_out_tiles(2)
    store(WOUT, gwo_out)
    b.r3(1, o, 3)
    spread_done("ctx", ctx_rows)
    w_proj_tiles()
    store(WPROJ, gwp_out)
    gl.sent()
    loads["wi"].wait()
    relay(("gh", 1), gh_rows(1))
    spread_done(("gh", 1), gh_rows(1))
    partials(0, o)
    for j in range(4):
        b.r4(1, o, j)
    spread_done(("gh", 0), gh_rows(0))
    red.s2(0, o, 0)
    red.s2(0, o, 1)
    partials(1, yh)
    red.s2(0, o, 2)
    red.s2(0, o, 3)
    ctx_done()
    red.s3(0, o, 0)
    red.s2(1, yh, 0)
    red.s3(0, o, 1)
    red.s3(0, o, 2)
    red.s2(1, yh, 1)
    red.t2(0, o)
    red.s3(0, o, 3)
    red.s2(1, yh, 2)
    red.s2(1, yh, 3)
    w_in_tiles(0, 2)
    for q in (0, 1):
        YS[:, pl.ds(q * red.width, red.width)] = red.t3(0, q)
    yl_links.send(("yh",), YS, YR, "yh")
    red.s3(1, yh, 0)
    w_in_tiles(2, 1)
    red.s3(1, yh, 1)
    red.s3(1, yh, 2)
    red.t2(1, yh)
    red.s3(1, yh, 3)
    w_in_tiles(3, 3)
    store(WIN2, gwi_out)
    yl_links.got(("yh",), YR)
    for q in (0, 1):
        cols = pl.ds(q * red.width, red.width)
        GN[:, cols] = (red.t3(1, q) + YR[:, cols]).astype(bf16)
    store(GN, gn_out)
    for links in (nl, yl_links, rl):
        links.sent()
    for s in stores:
        s.wait()


def body(normed, context, hidden_pre, grad_out, w_in, w_out, w_proj):
    block, width = grad_out.shape
    shard, hidden = hidden_pre.shape
    feats = context.shape[1]
    tokens = 32 * block
    chunk = 4 * block
    half = width // 2
    scratch = [
        pltpu.VMEM((tokens, width), bf16),
        pltpu.VMEM((tokens, width), bf16),
        pltpu.VMEM((tokens, hidden), bf16),
        pltpu.VMEM((tokens, feats), bf16),
        pltpu.VMEM((shard, hidden), bf16),
        pltpu.VMEM(w_in.shape, bf16),
        pltpu.VMEM(w_out.shape, bf16),
        pltpu.VMEM(w_proj.shape, bf16),
        pltpu.VMEM((tokens, hidden), bf16),
        pltpu.VMEM((shard, hidden), f32),
        pltpu.VMEM((2, 2, chunk, hidden), f32),
        pltpu.VMEM((2, 2, chunk, hidden), f32),
        pltpu.VMEM((2, chunk, hidden), f32),
        pltpu.VMEM((2, chunk, hidden), bf16),
        pltpu.VMEM((2, chunk, hidden), bf16),
        pltpu.VMEM((2, shard, feats), f32),
        pltpu.VMEM((2, shard, feats), f32),
        pltpu.VMEM((shard, feats), f32),
        pltpu.VMEM((shard, feats), bf16),
        pltpu.VMEM((shard, feats), bf16),
        pltpu.VMEM((2, 2, 4, 2, block, half // 2), bf16),
        pltpu.VMEM((2, 2, 4, 2, block, half), bf16),
        pltpu.VMEM((2, 2, 2, block, half // 2), bf16),
        pltpu.VMEM((2, 2, 2, block, half), bf16),
        pltpu.VMEM((2, 2, block, half), f32),
        pltpu.VMEM((block, width), f32),
        pltpu.VMEM((block, width), f32),
        pltpu.VMEM((block, width), bf16),
        pltpu.VMEM((shard, feats), bf16),
        pltpu.SemaphoreType.DMA((SEMS,)),
        pltpu.SemaphoreType.DMA((SEMS,)),
        pltpu.SemaphoreType.DMA((16,)),
    ]
    outs = [normed, context, w_in, w_out, w_proj]

    def call(*refs):
        kernel(1.0 / math.sqrt(tokens), *refs)

    return tuple(pl.pallas_call(
        call,
        out_shape=[jax.ShapeDtypeStruct(v.shape, v.dtype) for v in outs],
        in_specs=[pl.BlockSpec(memory_space=pl.ANY)] * 7,
        out_specs=[pl.BlockSpec(memory_space=pl.ANY)] * 5,
        scratch_shapes=scratch,
        compiler_params=pltpu.CompilerParams(
            collective_id=0, has_side_effects=True, vmem_limit_bytes=63 * 2**20),
    )(normed, context, hidden_pre, grad_out, w_in, w_out, w_proj))


def solution(mesh):
    in_specs = (
        P(("gx", "gy"), "gz"),
        P("gz", ("gx", "gy")),
        P("gz", ("gx", "gy")),
        P(("gx", "gy"), "gz"),
        P("gz", ("gx", "gy")),
        P(("gx", "gy"), "gz"),
        P(("gx", "gy"), "gz"),
    )
    out_specs = (
        P(("gx", "gy"), "gz"),
        P("gz", ("gx", "gy")),
        P("gz", ("gx", "gy")),
        P(("gx", "gy"), "gz"),
        P(("gx", "gy"), "gz"),
    )
    return jax.shard_map(body, mesh=mesh, in_specs=in_specs, out_specs=out_specs, check_vma=False)
```

```python
import math

import jax
import jax.numpy as jnp
from jax import lax
from jax.experimental import pallas as pl
from jax.experimental.pallas import tpu as pltpu
from jax.sharding import PartitionSpec as P

MESH = pl.DeviceIdType.MESH
f32, bf16 = jnp.float32, jnp.bfloat16
inv_root_two = 0.7071067811865476
inv_root_two_pi = 0.3989422804014327
SEMS = 352
K = dict(g=(1e9, 2.5), n=(2.5, 2.5), nx=(1, (("gh", 0, 1, "spread"),), 1e9), act=12, ctx=13, rs=(1e9, 1.0), ab=0.5, pieces=4)


def nt(left, right):
    return lax.dot_general(left, right, (((1,), (1,)), ((), ())), preferred_element_type=f32)


def nn(left, right):
    return lax.dot_general(left, right, (((1,), (0,)), ((), ())), preferred_element_type=f32)


def tn(left, right):
    return lax.dot_general(left, right, (((0,), (0,)), ((), ())), preferred_element_type=f32)


class Place:
    def __init__(self, block):
        gx, gy, gz = (lax.axis_index(a) for a in ("gx", "gy", "gz"))
        self.block = block
        self.z, self.yh, self.x, self.gz = gx // 2, lax.rem(gx, 2), gy, gz
        self.yl, self.c = gz // 2, lax.rem(gz, 2)
        z, yh, x = self.z, self.yh, self.x
        zp, zm, z2 = (lax.rem(z + k, 4) for k in (1, 3, 2))
        xp, xm, x2 = (lax.rem(x + k, 4) for k in (1, 3, 2))
        self.zs = (z, zp, zm, z2)
        self.xs = (x, xp, xm, x2)
        self.dev = {
            "x+": (gx, xp, gz),
            "x-": (gx, xm, gz),
            "z+": (zp * 2 + yh, x, gz),
            "z-": (zm * 2 + yh, x, gz),
            "yh": (z * 2 + 1 - yh, x, gz),
            "yl": (gx, gy, (1 - self.yl) * 2 + self.c),
            "c": (gx, gy, self.yl * 2 + 1 - self.c),
        }

    def rows(self, z, yh, x):
        return pl.ds(pl.multiple_of((z * 8 + yh * 4 + x) * self.block, self.block), self.block)

    def chunk(self, z, yh):
        n = 4 * self.block
        return pl.ds(pl.multiple_of((z * 2 + yh) * n, n), n)

    def shard(self, j):
        n = 8 * self.block
        return pl.ds(pl.multiple_of(j * n, n), n)


class Plan:
    rate = {"x+": 46e3, "x-": 46e3, "z+": 46e3, "z-": 46e3, "y": 46e3, "c": 6e5}
    latency = 1.5

    def __init__(self, place, send_sems, recv_sems):
        self.place, self.ss, self.rs = place, send_sems, recv_sems
        self.tasks, self.index, self.recv, self.local = {}, {}, {}, {}
        self.done, self.copies = set(), {}

    def load(self, key, copy, at):
        copy.start()
        self.local[key] = (copy, at)

    def add(self, name, prio, fn=None, needs=(), after=(), sends=(), dur=0.1, backlog=1e9):
        self.tasks[name] = (prio, fn, tuple(needs), tuple(after), tuple(sends), dur, backlog)
        for key, src, dst, to, here in sends:
            self.index[key] = len(self.index)
            self.recv[key] = here

    def order(self):
        arrive = {k: at for k, (_, at) in self.local.items()}
        free = dict.fromkeys(self.rate, 0.0)
        left, finished, now, out = dict(self.tasks), set(), 0.0, []
        self.log = []
        while left:
            ready, times = [], []
            for name, (prio, fn, needs, after, sends, dur, backlog) in left.items():
                if any(a not in finished for a in after) or any(k not in arrive for k in needs):
                    continue
                at = max([arrive[k] for k in needs], default=0.0)
                for s in sends:
                    at = max(at, free[self.link(s[3])] - backlog)
                if at <= now:
                    ready.append((prio, len(ready), name))
                else:
                    times.append(at)
            if not ready:
                now = min(times)
                continue
            name = min(ready)[2]
            prio, fn, needs, after, sends, dur, backlog = left.pop(name)
            self.log.append((now, name))
            now += dur
            for key, src, dst, to, here in sends:
                link = self.link(to)
                size = math.prod(here.shape) * jnp.dtype(here.dtype).itemsize
                free[link] = max(free[link], now) + size / self.rate[link]
                arrive[key] = free[link] + self.latency
            finished.add(name)
            out.append(name)
        self.log.append((max(now, max(free.values())), "end"))
        return out

    def link(self, to):
        return "y" if to in ("yl", "yh") else to

    def copy(self, key, src, dst, to):
        i = self.index[key]
        return pltpu.make_async_remote_copy(
            src_ref=src, dst_ref=dst, send_sem=self.ss.at[i], recv_sem=self.rs.at[i],
            device_id=self.place.dev[to], device_id_type=MESH)

    def wait(self, key):
        if key in self.done:
            return
        self.done.add(key)
        if key in self.local:
            self.local[key][0].wait()
        else:
            self.copy(key, self.recv[key], self.recv[key], "x+").wait_recv()

    def sent(self, keep):
        for key in [k for k in self.copies if keep(k)]:
            self.copies.pop(key).wait_send()

    def run(self):
        for name in self.order():
            prio, fn, needs, after, sends, dur, backlog = self.tasks[name]
            for k in needs:
                self.wait(k)
            if fn is not None:
                fn()
            for key, src, dst, to, here in sends:
                self.copies[key] = self.copy(key, src, dst, to)
                self.copies[key].start()
        for key in list(self.local) + list(self.index):
            self.wait(key)
        self.sent(lambda k: True)


WAYS = (("x+", "x-"), ("z+", "z-"))


def add_gather(plan, name, full, prio, backlogs, exchange):
    p = plan.place
    width = full.shape[1] // 2
    one, two = (p.xs, p.zs), (p.zs, p.xs)

    def view(part, yy, i, j, half=None):
        zz, xx = (j, i) if part == 0 else (i, j)
        start, n = part * width, width
        if half is not None:
            n = width // 2
            start += half * n
        return full.at[p.rows(zz, yy, xx), pl.ds(start, n)]

    own = full.at[p.rows(p.z, p.yh, p.x)]
    plan.add((name, "exchange"), exchange[0], needs=[("load", name)], after=exchange[1], backlog=exchange[2],
             sends=[((name, "y"), own, own, "yh", full.at[p.rows(p.z, 1 - p.yh, p.x)])])
    arrived = ([], [])
    for w, yy in ((0, p.yh), (1, 1 - p.yh)):
        pr = prio + w
        backlog = backlogs[w]
        start = [("load", name)] if w == 0 else [(name, "y")]
        got = arrived[w]

        def copy(key, v, to, here):
            return ((name, w) + key, v, v, to, here)

        firsts, seconds = [], []
        for q in (0, 1):
            i0, ip, im, i2 = one[q]
            j0, jp, jm, j2 = two[q]
            for s, near in ((0, im), (1, ip)):
                firsts.append(copy((q, "f", s), view(q, yy, i0, j0), WAYS[q][s], view(q, yy, near, j0)))
            for s, near in ((0, jm), (1, jp)):
                seconds.append(copy((q, 0, "s", s), view(q, yy, i0, j0), WAYS[1 - q][s], view(q, yy, i0, near)))
        plan.add((name, w, "firsts"), pr, needs=start, sends=firsts, backlog=backlog)
        plan.add((name, w, "seconds"), pr + 0.3, needs=start, sends=seconds, backlog=backlog)
        for q in (0, 1):
            i0, ip, im, i2 = one[q]
            j0, jp, jm, j2 = two[q]
            for s, i in ((0, im), (1, ip)):
                plan.add((name, w, q, "ff", s), pr, needs=[(name, w, q, "f", s)], backlog=backlog, sends=[
                    copy((q, "ff", s), view(q, yy, i, j0, s), WAYS[q][s], view(q, yy, i2, j0, s))])
            for k, i, needs in ((1, im, ["f0"]), (2, ip, ["f1"]), (3, i2, ["ff0", "ff1"])):
                plan.add((name, w, q, "s", k), pr + 0.2, needs=[(name, w, q, n[:-1], int(n[-1])) for n in needs],
                         backlog=backlog, sends=[
                    copy((q, k, "s", s), view(q, yy, i, j0), WAYS[1 - q][s], view(q, yy, i, near))
                    for s, near in ((0, jm), (1, jp))])
            for k, i in enumerate((i0, im, ip, i2)):
                for s, near in ((0, jm), (1, jp)):
                    plan.add((name, w, q, k, "sf", s), pr + 0.1, needs=[(name, w, q, k, "s", s)], backlog=backlog, sends=[
                        copy((q, k, "sf", s), view(q, yy, i, near, s), WAYS[1 - q][s], view(q, yy, i, j2, s))])
                    got += [(name, w, q, k, "s", s), (name, w, q, k, "sf", s)]
            got += [(name, w, q, "f", 0), (name, w, q, "f", 1), (name, w, q, "ff", 0), (name, w, q, "ff", 1)]
        got += start
    return arrived


def add_scatter(plan, d, far1, near1, far2, near2, keep, ys, yr, gn, prio, backlogs):
    p = plan.place
    width = d.shape[1] // 2
    one, two = (p.zs, p.xs), (p.xs, p.zs)

    def view(part, yy, i, j, half=None):
        zz, xx = (i, j) if part == 0 else (j, i)
        start, n = part * width, width
        if half is not None:
            n = width // 2
            start += half * n
        return d.at[p.rows(zz, yy, xx), pl.ds(start, n)]

    def fold(into, *terms):
        def fn():
            total = into[...].astype(f32)
            for t in terms:
                total = total + t[...].astype(f32)
            into[...] = total.astype(into.dtype)
        return fn

    for w, yy in ((0, 1 - p.yh), (1, p.yh)):
        pr = prio + w
        b = backlogs[w]
        for q in (0, 1):
            first, second = WAYS[1 - q], WAYS[q]
            j0, jp, jm, j2 = two[q]
            js = (j2, jp, jm, j0)
            slot = (3, 1, 2, 0)

            def part_of(i, k):
                return ("partial", w, i if q == 0 else slot[k])

            for k, j in enumerate(js):
                far = [("rs", w, q, "far1", k, h) for h in (0, 1)]
                near = [("rs", w, q, "near1", k, h) for h in (0, 1)]
                plan.add(("rs", w, q, "s1", k), pr + 0.1, after=[part_of(3, k)], backlog=b, sends=[
                    (far[h], view(q, yy, one[q][3], j, h), far1.at[w, q, k, h], first[h], far1.at[w, q, k, h])
                    for h in (0, 1)])
                for h in (0, 1):
                    i = 1 + h
                    plan.add(("rs", w, q, "s2", k, h), pr + 0.05 * k / 4, fold(view(q, yy, one[q][i], j, h), far1.at[w, q, k, h]),
                             needs=[far[h]], after=[part_of(i, k)], dur=0.15, backlog=b, sends=[
                        (near[h], view(q, yy, one[q][i], j), near1.at[w, q, k, h], first[h], near1.at[w, q, k, h])])
                mine = view(q, yy, one[q][0], j)
                if k < 3:
                    fn = fold(mine, near1.at[w, q, k, 0], near1.at[w, q, k, 1])
                else:
                    def fn(mine=mine, w=w, q=q, k=k):
                        keep[w, q] = (mine[...].astype(f32) + near1[w, q, k, 0].astype(f32)
                                      + near1[w, q, k, 1].astype(f32))
                plan.add(("rs", w, q, "s3", k), pr - 0.1, fn, needs=near, after=[part_of(0, k)], dur=0.25, sends=[
                    (("rs", w, q, "far2", h), view(q, yy, one[q][0], j, h), far2.at[w, q, h], second[h], far2.at[w, q, h])
                    for h in (0, 1)] if k == 0 else [])
            for h in (0, 1):
                plan.add(("rs", w, q, "t2", h), pr - 0.2, fold(view(q, yy, one[q][0], two[q][1 + h], h), far2.at[w, q, h]),
                         needs=[("rs", w, q, "far2", h)], after=[("rs", w, q, "s3", 1 + h)], dur=0.15, sends=[
                    (("rs", w, q, "near2", h), view(q, yy, one[q][0], two[q][1 + h]), near2.at[w, q, h], second[h],
                     near2.at[w, q, h])])
            cols = pl.ds(q * width, width)

            def total(w=w, q=q):
                return keep[w, q] + near2[w, q, 0].astype(f32) + near2[w, q, 1].astype(f32)

            needs = [("rs", w, q, "near2", h) for h in (0, 1)]
            if w == 0:
                def fn(total=total, cols=cols):
                    ys[:, cols] = total()
                plan.add(("rs", "yh", q), pr - 0.3, fn, needs=needs, after=[("rs", w, q, "s3", 3)], dur=0.2,
                         sends=[(("yh", q), ys.at[:, cols], yr.at[:, cols], "yh", yr.at[:, cols])])
            else:
                def fn(total=total, cols=cols):
                    gn[:, cols] = (total() + yr[:, cols]).astype(bf16)
                plan.add(("rs", "end", q), pr - 0.3, fn, needs=needs + [("yh", q)], after=[("rs", w, q, "s3", 3)], dur=0.2)


def kernel(scale, n_in, c_in, h_in, g_in, wi_in, wo_in, wp_in,
           gn_out, gc_out, gwi_out, gwo_out, gwp_out,
           G, N, ACT, CTX, HP, WIN, WOUT, WPROJ, GH, SLOPE, P1S, P1R, POWN, P2S, P2R,
           C1S, C1R, COWN, C2S, C2R, FAR1, NEAR1, FAR2, NEAR2, KEEP, YS, YR, ss, rs, ls):
    block = g_in.shape[0]
    p = Place(block)
    z, yh, x, gz, yl, c = p.z, p.yh, p.x, p.gz, p.yl, p.c
    o = 1 - yh
    n = 4 * block
    plan = Plan(p, ss, rs)
    other_y, other_c, other_yc = (1 - yl) * 2 + c, yl * 2 + 1 - c, (1 - yl) * 2 + 1 - c

    bar = pltpu.get_barrier_semaphore()
    for d in p.dev.values():
        pl.semaphore_signal(bar, inc=1, device_id=d, device_id_type=MESH)
    for i, (name, src, dst, at) in enumerate((
            ("g", g_in, G.at[p.rows(z, yh, x)], 0.0), ("h", h_in, HP, 0.0), ("c", c_in, CTX.at[gz], 0.0),
            ("n", n_in, N.at[p.rows(z, yh, x)], 0.0), ("wo", wo_in, WOUT, 1.0), ("wp", wp_in, WPROJ, 2.0),
            ("wi", wi_in, WIN, 3.0))):
        plan.load(("load", name), pltpu.make_async_copy(src, dst, ls.at[i]), at)
    pl.semaphore_wait(bar, len(p.dev))

    g_got = add_gather(plan, "g", G, 0, K["g"], (-1, (), 0.5))
    n_got = add_gather(plan, "n", N, 20, K["n"], K["nx"])

    def spread(key, view, prio, needs=(), after=(), fn=None, dur=0.1, backlog=1e9, relay=None):
        plan.add(key + ("spread",), prio, fn, needs=needs, after=after, dur=dur, backlog=backlog, sends=[
            (key + ("y",), view(gz), view(gz), "yl", view(other_y)),
            (key + ("c",), view(gz), view(gz), "c", view(other_c))])
        plan.add(key + ("relay",), prio + 0.1 if relay is None else relay, needs=[key + ("y",)], sends=[
            (key + ("cy",), view(other_y), view(other_y), "c", view(other_yc))])
        return [key + (k,) for k in ("y", "c", "cy")]

    act_got = []
    pieces = K["pieces"]
    half_rows = HP.shape[0] // pieces
    for half in range(pieces):
        def gelu(half=half):
            @pl.loop(0, half_rows // 16)
            def _(i):
                here = pl.ds(pl.multiple_of(half * half_rows + i * 16, 16), 16)
                v = HP[here, :].astype(f32)
                cdf = 0.5 * (1.0 + lax.erf(v * inv_root_two))
                density = jnp.exp(-0.5 * v * v) * inv_root_two_pi
                SLOPE[here, :] = cdf + v * density
                there = pl.ds(pl.multiple_of((gz * pieces + half) * half_rows + i * 16, 16), 16)
                ACT[there, :] = (v * cdf).astype(bf16)

        plan.add(("gelu", half), 1.5, gelu, needs=[("load", "h")], after=[("g", 0, "seconds")], dur=1.2 / pieces)
        act_got += spread(("act", half), lambda j, half=half: ACT.at[pl.ds(
            pl.multiple_of((j * pieces + half) * half_rows, half_rows), half_rows)], K["act"], after=[("gelu", half), ("g", "exchange")],
            backlog=K["ab"])
    ctx_got = spread(("ctx",), lambda j: CTX.at[j], K["ctx"], needs=[("load", "c")], after=[("g", "exchange")],
                     backlog=K["ab"])

    wave_yh = (yh, o)
    gh_got = ([], [])
    sub = n // 2
    for w in (0, 1):
        for s, yy in enumerate((1 - yl, yl)):
            def peer(w=w, s=s, yy=yy):
                P1S[w, s] = nt(G[p.chunk(yy * 2 + 1 - c, wave_yh[w]), :], WOUT[...])

            def own(w=w, s=s, yy=yy):
                v = nt(G[p.chunk(yy * 2 + c, wave_yh[w]), :], WOUT[...]) + P1R[w, s]
                if s == 0:
                    P2S[w] = v.astype(bf16)
                else:
                    POWN[w] = v

            plan.add(("p1", w, s), 3 + 0.1 * s, peer, needs=g_got[w] + [("load", "wo")], dur=0.95,
                     after=[("p1", w, 0)] if s else [], sends=[
                (("p1", w, s), P1S.at[w, s], P1R.at[w, s], "c", P1R.at[w, s])])
            plan.add(("own", w, s), 3.2 + 0.1 * s, own, needs=[("p1", w, s)], after=[("p1", w, 1)], dur=1.0, sends=[
                (("p2", w, h), P2S.at[w, pl.ds(h * sub, sub)], P2R.at[w, pl.ds(h * sub, sub)], "yl",
                 P2R.at[w, pl.ds(h * sub, sub)]) for h in (0, 1)] if s == 0 else [])
        for h in (0, 1):
            def hidden(w=w, h=h):
                here = pl.ds(h * sub, sub)
                local = pl.ds(pl.multiple_of(wave_yh[w] * n + h * sub, sub), sub)
                rows = pl.ds(pl.multiple_of((gz * 2 + wave_yh[w]) * n + h * sub, sub), sub)
                GH[rows, :] = ((POWN[w, here] + P2R[w, here].astype(f32)) * SLOPE[local, :]).astype(bf16)

            gh_got[w].extend(spread(("gh", w, h), lambda j, w=w, h=h: GH.at[pl.ds(
                pl.multiple_of((j * 2 + wave_yh[w]) * n + h * sub, sub), sub)], 2, fn=hidden, needs=[("p2", w, h)],
                after=[("own", w, 1)] + [("gelu", i) for i in range(pieces)], dur=0.3))

    g_all = g_got[0] + g_got[1]
    for s, yy in enumerate((1 - yl, yl)):
        def peer(s=s, yy=yy):
            C1S[s] = nt(WPROJ[...], G[p.shard(yy * 2 + 1 - c), :])

        def own(s=s, yy=yy):
            v = nt(WPROJ[...], G[p.shard(yy * 2 + c), :]) + C1R[s]
            if s == 0:
                C2S[...] = v.astype(bf16)
            else:
                COWN[...] = v

        plan.add(("c1", s), 30 + s, peer, needs=g_all + [("load", "wp")], dur=0.6,
                 after=[("c1", 0)] if s else [], sends=[
            (("c1", s), C1S.at[s], C1R.at[s], "c", C1R.at[s])])
        plan.add(("cown", s), 32 + s, own, needs=[("c1", s)], after=[("c1", 1)], dur=0.6)

    plan.add(("c2",), 60, needs=[], after=[("cown", 0), ("gh", 1, 0, "spread"), ("gh", 1, 1, "spread")],
             sends=[(("c2",), C2S, C2R, "yl", C2R)])

    def ctx_done():
        gc_out[...] = (COWN[...] + C2R[...].astype(f32)).astype(bf16)

    plan.add(("gc",), 70, ctx_done, needs=[("c2",)], after=[("cown", 1)], dur=0.1)

    readers = [("own", w, s) for w in (0, 1) for s in (0, 1)] + [("cown", 0), ("cown", 1)]
    for f in range(WOUT.shape[0] // 256):
        for t in range(3):
            def tile(f=f, t=t):
                rows, cols = pl.ds(f * 256, 256), pl.ds(t * 512, 512)
                gwo_out[rows, cols] = (tn(ACT[:, rows], G[:, cols]) * scale).astype(bf16)

            plan.add(("wo", f, t), 40, tile, needs=g_all + act_got, dur=0.75)
            readers.append(("wo", f, t))
    for t in range(3):
        def tile(t=t):
            cols = pl.ds(t * 512, 512)
            total = nn(CTX[0], G[p.shard(0), cols])
            for j in range(1, 4):
                total += nn(CTX[j], G[p.shard(j), cols])
            gwp_out[:, cols] = (total * scale).astype(bf16)

        plan.add(("wp", t), 46, tile, needs=g_all + ctx_got, dur=0.65)
    readers += [("wp", t) for t in range(3)]

    plan.add(("g", "sent"), 48, lambda: plan.sent(lambda k: k[0] == "g"), after=readers
             + [k for k in plan.tasks if k[0] == "g"], dur=0.1)
    for w, yy in ((0, o), (1, yh)):
        for i in (3, 1, 2, 0):
            def partial(i=i, yy=yy):
                rows = p.chunk(p.zs[i], yy)
                G[rows, :] = nt(GH[rows, :], WIN[...]).astype(bf16)

            plan.add(("partial", w, i), 4 + w * 8 + 0.01 * ((3, 1, 2, 0).index(i)), partial, needs=gh_got[1 - w] + [("load", "wi")],
                     after=[("g", "sent"), ("gh", 1 - w, 0, "spread"), ("gh", 1 - w, 1, "spread")], dur=1.0)
    add_scatter(plan, G, FAR1, NEAR1, FAR2, NEAR2, KEEP, YS, YR, gn_out, 7, K["rs"])

    parts = [("partial", w, i) for w in (0, 1) for i in range(4)]
    for t in range(N.shape[1] // 256):
        def tile(t=t):
            cols = pl.ds(t * 256, 256)
            gwi_out[cols, :] = (tn(N[:, cols], GH[...]) * scale).astype(bf16)

        plan.add(("wi", t), 80, tile, needs=n_got[0] + n_got[1], after=parts, dur=1.1)

    plan.run()


def copy_out(*refs):
    copies = [pltpu.make_async_copy(refs[i], refs[5 + i], refs[10].at[i]) for i in range(5)]
    for c in copies:
        c.start()
    for c in copies:
        c.wait()


def body(normed, context, hidden_pre, grad_out, w_in, w_out, w_proj):
    block, width = grad_out.shape
    shard, hidden = hidden_pre.shape
    feats = context.shape[1]
    tokens = 32 * block
    chunk = 4 * block
    half = width // 2
    scratch = [
        pltpu.VMEM((tokens, width), bf16),
        pltpu.VMEM((tokens, width), bf16),
        pltpu.VMEM((tokens, hidden), bf16),
        pltpu.VMEM((4, feats, shard), bf16),
        pltpu.VMEM((shard, hidden), bf16),
        pltpu.VMEM(w_in.shape, bf16),
        pltpu.VMEM(w_out.shape, bf16),
        pltpu.VMEM(w_proj.shape, bf16),
        pltpu.VMEM((tokens, hidden), bf16),
        pltpu.VMEM((shard, hidden), f32),
        pltpu.VMEM((2, 2, chunk, hidden), f32),
        pltpu.VMEM((2, 2, chunk, hidden), f32),
        pltpu.VMEM((2, chunk, hidden), f32),
        pltpu.VMEM((2, chunk, hidden), bf16),
        pltpu.VMEM((2, chunk, hidden), bf16),
        pltpu.VMEM((2, feats, shard), f32),
        pltpu.VMEM((2, feats, shard), f32),
        pltpu.VMEM((feats, shard), f32),
        pltpu.VMEM((feats, shard), bf16),
        pltpu.VMEM((feats, shard), bf16),
        pltpu.VMEM((2, 2, 4, 2, block, half // 2), bf16),
        pltpu.VMEM((2, 2, 4, 2, block, half), bf16),
        pltpu.VMEM((2, 2, 2, block, half // 2), bf16),
        pltpu.VMEM((2, 2, 2, block, half), bf16),
        pltpu.VMEM((2, 2, block, half), f32),
        pltpu.VMEM((block, width), f32),
        pltpu.VMEM((block, width), f32),
        pltpu.SemaphoreType.DMA((SEMS,)),
        pltpu.SemaphoreType.DMA((SEMS,)),
        pltpu.SemaphoreType.DMA((8,)),
    ]
    context = context.T
    outs = [normed, context, w_in, w_out, w_proj]

    def call(*refs):
        kernel(1.0 / math.sqrt(tokens), *refs)

    results = pl.pallas_call(
        call,
        out_shape=[pltpu.VMEM(v.shape, v.dtype) for v in outs],
        in_specs=[pl.BlockSpec(memory_space=pl.ANY)] * 7,
        out_specs=[pl.BlockSpec(memory_space=pltpu.VMEM)] * 5,
        scratch_shapes=scratch,
        compiler_params=pltpu.CompilerParams(
            collective_id=0, has_side_effects=True, vmem_limit_bytes=56 * 2**20),
    )(normed, context, hidden_pre, grad_out, w_in, w_out, w_proj)
    gn, gc, gwi, gwo, gwp = pl.pallas_call(
        copy_out,
        out_shape=[jax.ShapeDtypeStruct(v.shape, v.dtype) for v in outs],
        in_specs=[pl.BlockSpec(memory_space=pltpu.VMEM)] * 5,
        out_specs=[pl.BlockSpec(memory_space=pl.ANY)] * 5,
        scratch_shapes=[pltpu.SemaphoreType.DMA((5,))],
        compiler_params=pltpu.CompilerParams(vmem_limit_bytes=2**20),
    )(*results)
    return gn, gc.T, gwi, gwo, gwp


def solution(mesh):
    in_specs = (
        P(("gx", "gy"), "gz"),
        P("gz", ("gx", "gy")),
        P("gz", ("gx", "gy")),
        P(("gx", "gy"), "gz"),
        P("gz", ("gx", "gy")),
        P(("gx", "gy"), "gz"),
        P(("gx", "gy"), "gz"),
    )
    out_specs = (
        P(("gx", "gy"), "gz"),
        P("gz", ("gx", "gy")),
        P("gz", ("gx", "gy")),
        P(("gx", "gy"), "gz"),
        P(("gx", "gy"), "gz"),
    )
    return jax.shard_map(body, mesh=mesh, in_specs=in_specs, out_specs=out_specs, check_vma=False)
```

```python
import math

import jax
import jax.numpy as jnp
from jax import lax
from jax.experimental import pallas as pl
from jax.experimental.pallas import tpu as pltpu
from jax.sharding import PartitionSpec as P

MESH = pl.DeviceIdType.MESH
f32, bf16 = jnp.float32, jnp.bfloat16
inv_root_two = 0.7071067811865476
inv_root_two_pi = 0.3989422804014327
SEMS = 352
K = dict(g=(1e9, 2.5), n=(2.5, 2.5), nx=(1, (("gh", 0, 1, "spread"),), 1e9), act=12, ctx=13, rs=(1e9, 1.0), ab=0.5, pieces=4)

TUNE = {
    ('act', 'relay'): (-36.05, None),
    ('act', 'spread'): (2.79, 1.0),
    ('c1',): (-4.12, 1.5),
    ('c2',): (25.01, 0.5),
    ('cown',): (-9.27, 0.5),
    ('ctx', 'relay'): (-22.54, 0.5),
    ('ctx', 'spread'): (55.46, 1.5),
    ('g', 'exchange'): (9.02, 4.0),
    ('g', 'sent'): (-19.85, 0.5),
    ('g', 0, 'ff'): (-29.46, 4.0),
    ('g', 0, 'firsts'): (8.89, 3.0),
    ('g', 0, 's'): (-27.07, 2.5),
    ('g', 0, 'seconds'): (-3.13, 2.5),
    ('g', 0, 'sf'): (7.86, None),
    ('g', 1, 'ff'): (7.52, 6.0),
    ('g', 1, 'firsts'): (13.91, None),
    ('g', 1, 's'): (12.11, 1.0),
    ('g', 1, 'seconds'): (5.76, 2.5),
    ('g', 1, 'sf'): (-40.36, 1e9),
    ('gc',): (-24.56, None),
    ('gelu',): (-13.85, 2.5),
    ('gh', 0, 'relay'): (30.97, 3.0),
    ('gh', 0, 'spread'): (-14.58, 3.0),
    ('gh', 1, 'relay'): (-20.72, None),
    ('gh', 1, 'spread'): (17.11, 4.0),
    ('n', 'exchange'): (26.73, 4.0),
    ('n', 0, 'ff'): (16.27, 4.0),
    ('n', 0, 'firsts'): (-3.65, 1.0),
    ('n', 0, 's'): (-21.35, 0.5),
    ('n', 0, 'seconds'): (1.58, 3.0),
    ('n', 0, 'sf'): (15.74, None),
    ('n', 1, 'ff'): (-58.75, 2.0),
    ('n', 1, 'firsts'): (-1.73, 1.0),
    ('n', 1, 's'): (-16.0, 3.0),
    ('n', 1, 'seconds'): (0.81, 6.0),
    ('n', 1, 'sf'): (-18.02, None),
    ('own', 0): (-4.16, 1.5),
    ('own', 1): (33.36, 2.5),
    ('p1', 0): (-37.69, 4.0),
    ('p1', 1): (-22.43, None),
    ('partial', 0): (45.97, 6.0),
    ('partial', 1): (-1.22, 2.0),
    ('rs', 'end'): (39.5, 2.0),
    ('rs', 'yh'): (-20.47, 2.5),
    ('rs', 0, 's1'): (-22.5, None),
    ('rs', 0, 's2'): (-37.73, None),
    ('rs', 0, 's3'): (17.91, 6.0),
    ('rs', 0, 't2'): (-5.6, 2.5),
    ('rs', 1, 's1'): (-6.41, 4.0),
    ('rs', 1, 's2'): (-3.32, 0.5),
    ('rs', 1, 's3'): (-1.37, None),
    ('rs', 1, 't2'): (32.44, None),
    ('wi',): (25.65, 2.0),
    ('wo',): (1.57, 1.5),
    ('wp',): (38.35, 1.0),
}
LATENCY, STRETCH, PER_COPY = 2.235, 1.417, 0.03


def group(n):
    if n[0] in ("g", "n"):
        if len(n) <= 3:
            return n
        return (n[0], n[1], n[3] if n[3] in ("ff", "s") else n[4])
    if n[0] == "rs":
        return n[:2] if n[1] in ("yh", "end") else ("rs", n[1], n[3])
    if n[0] == "gh":
        return ("gh", n[1], n[3])
    if n[0] == "act":
        return ("act", n[2])
    if n[0] in ("partial", "p1", "own"):
        return n[:2]
    return n[:1] if n[0] in ("wo", "wp", "wi", "c1", "cown", "gelu") else n


def nt(left, right):
    return lax.dot_general(left, right, (((1,), (1,)), ((), ())), preferred_element_type=f32)


def nn(left, right):
    return lax.dot_general(left, right, (((1,), (0,)), ((), ())), preferred_element_type=f32)


def tn(left, right):
    return lax.dot_general(left, right, (((0,), (0,)), ((), ())), preferred_element_type=f32)


class Place:
    def __init__(self, block):
        gx, gy, gz = (lax.axis_index(a) for a in ("gx", "gy", "gz"))
        self.block = block
        self.z, self.yh, self.x, self.gz = gx // 2, lax.rem(gx, 2), gy, gz
        self.yl, self.c = gz // 2, lax.rem(gz, 2)
        z, yh, x = self.z, self.yh, self.x
        zp, zm, z2 = (lax.rem(z + k, 4) for k in (1, 3, 2))
        xp, xm, x2 = (lax.rem(x + k, 4) for k in (1, 3, 2))
        self.zs = (z, zp, zm, z2)
        self.xs = (x, xp, xm, x2)
        self.dev = {
            "x+": (gx, xp, gz),
            "x-": (gx, xm, gz),
            "z+": (zp * 2 + yh, x, gz),
            "z-": (zm * 2 + yh, x, gz),
            "yh": (z * 2 + 1 - yh, x, gz),
            "yl": (gx, gy, (1 - self.yl) * 2 + self.c),
            "c": (gx, gy, self.yl * 2 + 1 - self.c),
        }

    def rows(self, z, yh, x):
        return pl.ds(pl.multiple_of((z * 8 + yh * 4 + x) * self.block, self.block), self.block)

    def chunk(self, z, yh):
        n = 4 * self.block
        return pl.ds(pl.multiple_of((z * 2 + yh) * n, n), n)

    def shard(self, j):
        n = 8 * self.block
        return pl.ds(pl.multiple_of(j * n, n), n)


class Plan:
    rate = {"x+": 46e3, "x-": 46e3, "z+": 46e3, "z-": 46e3, "y": 46e3, "c": 6e5}
    latency = LATENCY

    def __init__(self, place, send_sems, recv_sems):
        self.place, self.ss, self.rs = place, send_sems, recv_sems
        self.tasks, self.index, self.recv, self.local = {}, {}, {}, {}
        self.done, self.copies = set(), {}

    def load(self, key, copy, at):
        copy.start()
        self.local[key] = (copy, at)

    def add(self, name, prio, fn=None, needs=(), after=(), sends=(), dur=0.1, backlog=1e9):
        shift, queue = TUNE.get(group(name), (0.0, None))
        prio, backlog = prio + shift, backlog if queue is None else queue
        self.tasks[name] = (prio, fn, tuple(needs), tuple(after), tuple(sends), dur, backlog)
        for key, src, dst, to, here in sends:
            self.index[key] = len(self.index)
            self.recv[key] = here

    def order(self):
        arrive = {k: at for k, (_, at) in self.local.items()}
        free = dict.fromkeys(self.rate, 0.0)
        left, finished, now, out = dict(self.tasks), set(), 0.0, []
        self.log = []
        while left:
            ready, times = [], []
            for name, (prio, fn, needs, after, sends, dur, backlog) in left.items():
                if any(a not in finished for a in after) or any(k not in arrive for k in needs):
                    continue
                at = max([arrive[k] for k in needs], default=0.0)
                for s in sends:
                    at = max(at, free[self.link(s[3])] - backlog)
                if at <= now:
                    ready.append((prio, len(ready), name))
                else:
                    times.append(at)
            if not ready:
                now = min(times)
                continue
            name = min(ready)[2]
            prio, fn, needs, after, sends, dur, backlog = left.pop(name)
            self.log.append((now, name))
            now += dur * STRETCH
            for key, src, dst, to, here in sends:
                link = self.link(to)
                size = math.prod(here.shape) * jnp.dtype(here.dtype).itemsize
                free[link] = max(free[link], now) + size / self.rate[link] + PER_COPY
                arrive[key] = free[link] + self.latency
            finished.add(name)
            out.append(name)
        self.log.append((max(now, max(free.values())), "end"))
        return out

    def link(self, to):
        return "y" if to in ("yl", "yh") else to

    def copy(self, key, src, dst, to):
        i = self.index[key]
        return pltpu.make_async_remote_copy(
            src_ref=src, dst_ref=dst, send_sem=self.ss.at[i], recv_sem=self.rs.at[i],
            device_id=self.place.dev[to], device_id_type=MESH)

    def wait(self, key):
        if key in self.done:
            return
        self.done.add(key)
        if key in self.local:
            self.local[key][0].wait()
        else:
            self.copy(key, self.recv[key], self.recv[key], "x+").wait_recv()

    def sent(self, keep):
        for key in [k for k in self.copies if keep(k)]:
            self.copies.pop(key).wait_send()

    def run(self):
        for name in self.order():
            prio, fn, needs, after, sends, dur, backlog = self.tasks[name]
            for k in needs:
                self.wait(k)
            if fn is not None:
                fn()
            for key, src, dst, to, here in sends:
                self.copies[key] = self.copy(key, src, dst, to)
                self.copies[key].start()
        for key in list(self.local) + list(self.index):
            self.wait(key)
        self.sent(lambda k: True)


WAYS = (("x+", "x-"), ("z+", "z-"))


def add_gather(plan, name, full, prio, backlogs, exchange):
    p = plan.place
    width = full.shape[1] // 2
    one, two = (p.xs, p.zs), (p.zs, p.xs)

    def view(part, yy, i, j, half=None):
        zz, xx = (j, i) if part == 0 else (i, j)
        start, n = part * width, width
        if half is not None:
            n = width // 2
            start += half * n
        return full.at[p.rows(zz, yy, xx), pl.ds(start, n)]

    own = full.at[p.rows(p.z, p.yh, p.x)]
    plan.add((name, "exchange"), exchange[0], needs=[("load", name)], after=exchange[1], backlog=exchange[2],
             sends=[((name, "y"), own, own, "yh", full.at[p.rows(p.z, 1 - p.yh, p.x)])])
    arrived = ([], [])
    for w, yy in ((0, p.yh), (1, 1 - p.yh)):
        pr = prio + w
        backlog = backlogs[w]
        start = [("load", name)] if w == 0 else [(name, "y")]
        got = arrived[w]

        def copy(key, v, to, here):
            return ((name, w) + key, v, v, to, here)

        firsts, seconds = [], []
        for q in (0, 1):
            i0, ip, im, i2 = one[q]
            j0, jp, jm, j2 = two[q]
            for s, near in ((0, im), (1, ip)):
                firsts.append(copy((q, "f", s), view(q, yy, i0, j0), WAYS[q][s], view(q, yy, near, j0)))
            for s, near in ((0, jm), (1, jp)):
                seconds.append(copy((q, 0, "s", s), view(q, yy, i0, j0), WAYS[1 - q][s], view(q, yy, i0, near)))
        plan.add((name, w, "firsts"), pr, needs=start, sends=firsts, backlog=backlog)
        plan.add((name, w, "seconds"), pr + 0.3, needs=start, sends=seconds, backlog=backlog)
        for q in (0, 1):
            i0, ip, im, i2 = one[q]
            j0, jp, jm, j2 = two[q]
            for s, i in ((0, im), (1, ip)):
                plan.add((name, w, q, "ff", s), pr, needs=[(name, w, q, "f", s)], backlog=backlog, sends=[
                    copy((q, "ff", s), view(q, yy, i, j0, s), WAYS[q][s], view(q, yy, i2, j0, s))])
            for k, i, needs in ((1, im, ["f0"]), (2, ip, ["f1"]), (3, i2, ["ff0", "ff1"])):
                plan.add((name, w, q, "s", k), pr + 0.2, needs=[(name, w, q, n[:-1], int(n[-1])) for n in needs],
                         backlog=backlog, sends=[
                    copy((q, k, "s", s), view(q, yy, i, j0), WAYS[1 - q][s], view(q, yy, i, near))
                    for s, near in ((0, jm), (1, jp))])
            for k, i in enumerate((i0, im, ip, i2)):
                for s, near in ((0, jm), (1, jp)):
                    plan.add((name, w, q, k, "sf", s), pr + 0.1, needs=[(name, w, q, k, "s", s)], backlog=backlog, sends=[
                        copy((q, k, "sf", s), view(q, yy, i, near, s), WAYS[1 - q][s], view(q, yy, i, j2, s))])
                    got += [(name, w, q, k, "s", s), (name, w, q, k, "sf", s)]
            got += [(name, w, q, "f", 0), (name, w, q, "f", 1), (name, w, q, "ff", 0), (name, w, q, "ff", 1)]
        got += start
    return arrived


def add_scatter(plan, d, far1, near1, far2, near2, keep, ys, yr, gn, prio, backlogs):
    p = plan.place
    width = d.shape[1] // 2
    one, two = (p.zs, p.xs), (p.xs, p.zs)

    def view(part, yy, i, j, half=None):
        zz, xx = (i, j) if part == 0 else (j, i)
        start, n = part * width, width
        if half is not None:
            n = width // 2
            start += half * n
        return d.at[p.rows(zz, yy, xx), pl.ds(start, n)]

    def fold(into, *terms):
        def fn():
            total = into[...].astype(f32)
            for t in terms:
                total = total + t[...].astype(f32)
            into[...] = total.astype(into.dtype)
        return fn

    for w, yy in ((0, 1 - p.yh), (1, p.yh)):
        pr = prio + w
        b = backlogs[w]
        for q in (0, 1):
            first, second = WAYS[1 - q], WAYS[q]
            j0, jp, jm, j2 = two[q]
            js = (j2, jp, jm, j0)
            slot = (3, 1, 2, 0)

            def part_of(i, k):
                return ("partial", w, i if q == 0 else slot[k])

            for k, j in enumerate(js):
                far = [("rs", w, q, "far1", k, h) for h in (0, 1)]
                near = [("rs", w, q, "near1", k, h) for h in (0, 1)]
                plan.add(("rs", w, q, "s1", k), pr + 0.1, after=[part_of(3, k)], backlog=b, sends=[
                    (far[h], view(q, yy, one[q][3], j, h), far1.at[w, q, k, h], first[h], far1.at[w, q, k, h])
                    for h in (0, 1)])
                for h in (0, 1):
                    i = 1 + h
                    plan.add(("rs", w, q, "s2", k, h), pr + 0.05 * k / 4, fold(view(q, yy, one[q][i], j, h), far1.at[w, q, k, h]),
                             needs=[far[h]], after=[part_of(i, k)], dur=0.15, backlog=b, sends=[
                        (near[h], view(q, yy, one[q][i], j), near1.at[w, q, k, h], first[h], near1.at[w, q, k, h])])
                mine = view(q, yy, one[q][0], j)
                if k < 3:
                    fn = fold(mine, near1.at[w, q, k, 0], near1.at[w, q, k, 1])
                else:
                    def fn(mine=mine, w=w, q=q, k=k):
                        keep[w, q] = (mine[...].astype(f32) + near1[w, q, k, 0].astype(f32)
                                      + near1[w, q, k, 1].astype(f32))
                plan.add(("rs", w, q, "s3", k), pr - 0.1, fn, needs=near, after=[part_of(0, k)], dur=0.25, sends=[
                    (("rs", w, q, "far2", h), view(q, yy, one[q][0], j, h), far2.at[w, q, h], second[h], far2.at[w, q, h])
                    for h in (0, 1)] if k == 0 else [])
            for h in (0, 1):
                plan.add(("rs", w, q, "t2", h), pr - 0.2, fold(view(q, yy, one[q][0], two[q][1 + h], h), far2.at[w, q, h]),
                         needs=[("rs", w, q, "far2", h)], after=[("rs", w, q, "s3", 1 + h)], dur=0.15, sends=[
                    (("rs", w, q, "near2", h), view(q, yy, one[q][0], two[q][1 + h]), near2.at[w, q, h], second[h],
                     near2.at[w, q, h])])
            cols = pl.ds(q * width, width)

            def total(w=w, q=q):
                return keep[w, q] + near2[w, q, 0].astype(f32) + near2[w, q, 1].astype(f32)

            needs = [("rs", w, q, "near2", h) for h in (0, 1)]
            if w == 0:
                def fn(total=total, cols=cols):
                    ys[:, cols] = total()
                plan.add(("rs", "yh", q), pr - 0.3, fn, needs=needs, after=[("rs", w, q, "s3", 3)], dur=0.2,
                         sends=[(("yh", q), ys.at[:, cols], yr.at[:, cols], "yh", yr.at[:, cols])])
            else:
                def fn(total=total, cols=cols):
                    gn[:, cols] = (total() + yr[:, cols]).astype(bf16)
                plan.add(("rs", "end", q), pr - 0.3, fn, needs=needs + [("yh", q)], after=[("rs", w, q, "s3", 3)], dur=0.2)


def kernel(scale, n_in, c_in, h_in, g_in, wi_in, wo_in, wp_in,
           gn_out, gc_out, gwi_out, gwo_out, gwp_out,
           G, N, ACT, CTX, HP, WIN, WOUT, WPROJ, GH, SLOPE, P1S, P1R, POWN, P2S, P2R,
           C1S, C1R, COWN, C2S, C2R, FAR1, NEAR1, FAR2, NEAR2, KEEP, YS, YR, ss, rs, ls):
    block = g_in.shape[0]
    p = Place(block)
    z, yh, x, gz, yl, c = p.z, p.yh, p.x, p.gz, p.yl, p.c
    o = 1 - yh
    n = 4 * block
    plan = Plan(p, ss, rs)
    other_y, other_c, other_yc = (1 - yl) * 2 + c, yl * 2 + 1 - c, (1 - yl) * 2 + 1 - c

    bar = pltpu.get_barrier_semaphore()
    for d in p.dev.values():
        pl.semaphore_signal(bar, inc=1, device_id=d, device_id_type=MESH)
    for i, (name, src, dst, at) in enumerate((
            ("g", g_in, G.at[p.rows(z, yh, x)], 0.0), ("h", h_in, HP, 0.0), ("c", c_in, CTX.at[gz], 0.0),
            ("n", n_in, N.at[p.rows(z, yh, x)], 0.0), ("wo", wo_in, WOUT, 1.0), ("wp", wp_in, WPROJ, 2.0),
            ("wi", wi_in, WIN, 3.0))):
        plan.load(("load", name), pltpu.make_async_copy(src, dst, ls.at[i]), at)
    pl.semaphore_wait(bar, len(p.dev))

    g_got = add_gather(plan, "g", G, 0, K["g"], (-1, (), 0.5))
    n_got = add_gather(plan, "n", N, 20, K["n"], K["nx"])

    def spread(key, view, prio, needs=(), after=(), fn=None, dur=0.1, backlog=1e9, relay=None):
        plan.add(key + ("spread",), prio, fn, needs=needs, after=after, dur=dur, backlog=backlog, sends=[
            (key + ("y",), view(gz), view(gz), "yl", view(other_y)),
            (key + ("c",), view(gz), view(gz), "c", view(other_c))])
        plan.add(key + ("relay",), prio + 0.1 if relay is None else relay, needs=[key + ("y",)], sends=[
            (key + ("cy",), view(other_y), view(other_y), "c", view(other_yc))])
        return [key + (k,) for k in ("y", "c", "cy")]

    act_got = []
    pieces = K["pieces"]
    half_rows = HP.shape[0] // pieces
    for half in range(pieces):
        def gelu(half=half):
            @pl.loop(0, half_rows // 16)
            def _(i):
                here = pl.ds(pl.multiple_of(half * half_rows + i * 16, 16), 16)
                v = HP[here, :].astype(f32)
                cdf = 0.5 * (1.0 + lax.erf(v * inv_root_two))
                density = jnp.exp(-0.5 * v * v) * inv_root_two_pi
                SLOPE[here, :] = cdf + v * density
                there = pl.ds(pl.multiple_of((gz * pieces + half) * half_rows + i * 16, 16), 16)
                ACT[there, :] = (v * cdf).astype(bf16)

        plan.add(("gelu", half), 1.5, gelu, needs=[("load", "h")], after=[("g", 0, "seconds")], dur=1.2 / pieces)
        act_got += spread(("act", half), lambda j, half=half: ACT.at[pl.ds(
            pl.multiple_of((j * pieces + half) * half_rows, half_rows), half_rows)], K["act"], after=[("gelu", half), ("g", "exchange")],
            backlog=K["ab"])
    ctx_got = spread(("ctx",), lambda j: CTX.at[j], K["ctx"], needs=[("load", "c")], after=[("g", "exchange")],
                     backlog=K["ab"])

    wave_yh = (yh, o)
    gh_got = ([], [])
    sub = n // 2
    for w in (0, 1):
        for s, yy in enumerate((1 - yl, yl)):
            def peer(w=w, s=s, yy=yy):
                P1S[w, s] = nt(G[p.chunk(yy * 2 + 1 - c, wave_yh[w]), :], WOUT[...])

            def own(w=w, s=s, yy=yy):
                v = nt(G[p.chunk(yy * 2 + c, wave_yh[w]), :], WOUT[...]) + P1R[w, s]
                if s == 0:
                    P2S[w] = v.astype(bf16)
                else:
                    POWN[w] = v

            plan.add(("p1", w, s), 3 + 0.1 * s, peer, needs=g_got[w] + [("load", "wo")], dur=0.95,
                     after=[("p1", w, 0)] if s else [], sends=[
                (("p1", w, s), P1S.at[w, s], P1R.at[w, s], "c", P1R.at[w, s])])
            plan.add(("own", w, s), 3.2 + 0.1 * s, own, needs=[("p1", w, s)], after=[("p1", w, 1)], dur=1.0, sends=[
                (("p2", w, h), P2S.at[w, pl.ds(h * sub, sub)], P2R.at[w, pl.ds(h * sub, sub)], "yl",
                 P2R.at[w, pl.ds(h * sub, sub)]) for h in (0, 1)] if s == 0 else [])
        for h in (0, 1):
            def hidden(w=w, h=h):
                here = pl.ds(h * sub, sub)
                local = pl.ds(pl.multiple_of(wave_yh[w] * n + h * sub, sub), sub)
                rows = pl.ds(pl.multiple_of((gz * 2 + wave_yh[w]) * n + h * sub, sub), sub)
                GH[rows, :] = ((POWN[w, here] + P2R[w, here].astype(f32)) * SLOPE[local, :]).astype(bf16)

            gh_got[w].extend(spread(("gh", w, h), lambda j, w=w, h=h: GH.at[pl.ds(
                pl.multiple_of((j * 2 + wave_yh[w]) * n + h * sub, sub), sub)], 2, fn=hidden, needs=[("p2", w, h)],
                after=[("own", w, 1)] + [("gelu", i) for i in range(pieces)], dur=0.3))

    g_all = g_got[0] + g_got[1]
    for s, yy in enumerate((1 - yl, yl)):
        def peer(s=s, yy=yy):
            C1S[s] = nt(WPROJ[...], G[p.shard(yy * 2 + 1 - c), :])

        def own(s=s, yy=yy):
            v = nt(WPROJ[...], G[p.shard(yy * 2 + c), :]) + C1R[s]
            if s == 0:
                C2S[...] = v.astype(bf16)
            else:
                COWN[...] = v

        plan.add(("c1", s), 30 + s, peer, needs=g_all + [("load", "wp")], dur=0.6,
                 after=[("c1", 0)] if s else [], sends=[
            (("c1", s), C1S.at[s], C1R.at[s], "c", C1R.at[s])])
        plan.add(("cown", s), 32 + s, own, needs=[("c1", s)], after=[("c1", 1)], dur=0.6)

    plan.add(("c2",), 60, needs=[], after=[("cown", 0), ("gh", 1, 0, "spread"), ("gh", 1, 1, "spread")],
             sends=[(("c2",), C2S, C2R, "yl", C2R)])

    def ctx_done():
        gc_out[...] = (COWN[...] + C2R[...].astype(f32)).astype(bf16)

    plan.add(("gc",), 70, ctx_done, needs=[("c2",)], after=[("cown", 1)], dur=0.1)

    readers = [("own", w, s) for w in (0, 1) for s in (0, 1)] + [("cown", 0), ("cown", 1)]
    for f in range(WOUT.shape[0] // 256):
        for t in range(3):
            def tile(f=f, t=t):
                rows, cols = pl.ds(f * 256, 256), pl.ds(t * 512, 512)
                gwo_out[rows, cols] = (tn(ACT[:, rows], G[:, cols]) * scale).astype(bf16)

            plan.add(("wo", f, t), 40, tile, needs=g_all + act_got, dur=0.75)
            readers.append(("wo", f, t))
    for t in range(3):
        def tile(t=t):
            cols = pl.ds(t * 512, 512)
            total = nn(CTX[0], G[p.shard(0), cols])
            for j in range(1, 4):
                total += nn(CTX[j], G[p.shard(j), cols])
            gwp_out[:, cols] = (total * scale).astype(bf16)

        plan.add(("wp", t), 46, tile, needs=g_all + ctx_got, dur=0.65)
    readers += [("wp", t) for t in range(3)]

    plan.add(("g", "sent"), 48, lambda: plan.sent(lambda k: k[0] == "g"), after=readers
             + [k for k in plan.tasks if k[0] == "g"], dur=0.1)
    for w, yy in ((0, o), (1, yh)):
        for i in (3, 1, 2, 0):
            def partial(i=i, yy=yy):
                rows = p.chunk(p.zs[i], yy)
                G[rows, :] = nt(GH[rows, :], WIN[...]).astype(bf16)

            plan.add(("partial", w, i), 4 + w * 8 + 0.01 * ((3, 1, 2, 0).index(i)), partial, needs=gh_got[1 - w] + [("load", "wi")],
                     after=[("g", "sent"), ("gh", 1 - w, 0, "spread"), ("gh", 1 - w, 1, "spread")], dur=1.0)
    add_scatter(plan, G, FAR1, NEAR1, FAR2, NEAR2, KEEP, YS, YR, gn_out, 7, K["rs"])

    parts = [("partial", w, i) for w in (0, 1) for i in range(4)]
    for t in range(N.shape[1] // 256):
        def tile(t=t):
            cols = pl.ds(t * 256, 256)
            gwi_out[cols, :] = (tn(N[:, cols], GH[...]) * scale).astype(bf16)

        plan.add(("wi", t), 80, tile, needs=n_got[0] + n_got[1], after=parts, dur=1.1)

    plan.run()


def copy_out(*refs):
    copies = [pltpu.make_async_copy(refs[i], refs[5 + i], refs[10].at[i]) for i in range(5)]
    for c in copies:
        c.start()
    for c in copies:
        c.wait()


def body(normed, context, hidden_pre, grad_out, w_in, w_out, w_proj):
    block, width = grad_out.shape
    shard, hidden = hidden_pre.shape
    feats = context.shape[1]
    tokens = 32 * block
    chunk = 4 * block
    half = width // 2
    scratch = [
        pltpu.VMEM((tokens, width), bf16),
        pltpu.VMEM((tokens, width), bf16),
        pltpu.VMEM((tokens, hidden), bf16),
        pltpu.VMEM((4, feats, shard), bf16),
        pltpu.VMEM((shard, hidden), bf16),
        pltpu.VMEM(w_in.shape, bf16),
        pltpu.VMEM(w_out.shape, bf16),
        pltpu.VMEM(w_proj.shape, bf16),
        pltpu.VMEM((tokens, hidden), bf16),
        pltpu.VMEM((shard, hidden), f32),
        pltpu.VMEM((2, 2, chunk, hidden), f32),
        pltpu.VMEM((2, 2, chunk, hidden), f32),
        pltpu.VMEM((2, chunk, hidden), f32),
        pltpu.VMEM((2, chunk, hidden), bf16),
        pltpu.VMEM((2, chunk, hidden), bf16),
        pltpu.VMEM((2, feats, shard), f32),
        pltpu.VMEM((2, feats, shard), f32),
        pltpu.VMEM((feats, shard), f32),
        pltpu.VMEM((feats, shard), bf16),
        pltpu.VMEM((feats, shard), bf16),
        pltpu.VMEM((2, 2, 4, 2, block, half // 2), bf16),
        pltpu.VMEM((2, 2, 4, 2, block, half), bf16),
        pltpu.VMEM((2, 2, 2, block, half // 2), bf16),
        pltpu.VMEM((2, 2, 2, block, half), bf16),
        pltpu.VMEM((2, 2, block, half), f32),
        pltpu.VMEM((block, width), f32),
        pltpu.VMEM((block, width), f32),
        pltpu.SemaphoreType.DMA((SEMS,)),
        pltpu.SemaphoreType.DMA((SEMS,)),
        pltpu.SemaphoreType.DMA((8,)),
    ]
    context = context.T
    outs = [normed, context, w_in, w_out, w_proj]

    def call(*refs):
        kernel(1.0 / math.sqrt(tokens), *refs)

    results = pl.pallas_call(
        call,
        out_shape=[pltpu.VMEM(v.shape, v.dtype) for v in outs],
        in_specs=[pl.BlockSpec(memory_space=pl.ANY)] * 7,
        out_specs=[pl.BlockSpec(memory_space=pltpu.VMEM)] * 5,
        scratch_shapes=scratch,
        compiler_params=pltpu.CompilerParams(
            collective_id=0, has_side_effects=True, vmem_limit_bytes=56 * 2**20),
    )(normed, context, hidden_pre, grad_out, w_in, w_out, w_proj)
    gn, gc, gwi, gwo, gwp = pl.pallas_call(
        copy_out,
        out_shape=[jax.ShapeDtypeStruct(v.shape, v.dtype) for v in outs],
        in_specs=[pl.BlockSpec(memory_space=pltpu.VMEM)] * 5,
        out_specs=[pl.BlockSpec(memory_space=pl.ANY)] * 5,
        scratch_shapes=[pltpu.SemaphoreType.DMA((5,))],
        compiler_params=pltpu.CompilerParams(vmem_limit_bytes=2**20),
    )(*results)
    return gn, gc.T, gwi, gwo, gwp


def solution(mesh):
    in_specs = (
        P(("gx", "gy"), "gz"),
        P("gz", ("gx", "gy")),
        P("gz", ("gx", "gy")),
        P(("gx", "gy"), "gz"),
        P("gz", ("gx", "gy")),
        P(("gx", "gy"), "gz"),
        P(("gx", "gy"), "gz"),
    )
    out_specs = (
        P(("gx", "gy"), "gz"),
        P("gz", ("gx", "gy")),
        P("gz", ("gx", "gy")),
        P(("gx", "gy"), "gz"),
        P(("gx", "gy"), "gz"),
    )
    return jax.shard_map(body, mesh=mesh, in_specs=in_specs, out_specs=out_specs, check_vma=False)
```

```python
import math

import jax
import jax.numpy as jnp
from jax import lax
from jax.experimental import pallas as pl
from jax.experimental.pallas import tpu as pltpu
from jax.sharding import PartitionSpec as P

MESH = pl.DeviceIdType.MESH
f32, bf16 = jnp.float32, jnp.bfloat16
inv_root_two = 0.7071067811865476
inv_root_two_pi = 0.3989422804014327
SEMS = 352
K = dict(g=(1e9, 2.5), n=(2.5, 2.5), nx=(1, (("gh", 0, 1, "spread"),), 1e9), act=12, ctx=13, rs=(1e9, 1.0), ab=0.5, pieces=4)

TUNE = {
    ('act', 'relay'): (-36.05, None),
    ('act', 'spread'): (2.79, 1.0),
    ('c1',): (-4.12, 1.5),
    ('c2',): (25.01, 0.5),
    ('cown',): (-9.27, 0.5),
    ('ctx', 'relay'): (-22.54, 0.5),
    ('ctx', 'spread'): (55.46, 1.5),
    ('g', 'exchange'): (9.02, 4.0),
    ('g', 'sent'): (-19.85, 0.5),
    ('g', 0, 'ff'): (-29.46, 4.0),
    ('g', 0, 'firsts'): (8.89, 3.0),
    ('g', 0, 's'): (-27.07, 2.5),
    ('g', 0, 'seconds'): (-3.13, 2.5),
    ('g', 0, 'sf'): (7.86, None),
    ('g', 1, 'ff'): (7.52, 6.0),
    ('g', 1, 'firsts'): (13.91, None),
    ('g', 1, 's'): (12.11, 1.0),
    ('g', 1, 'seconds'): (5.76, 2.5),
    ('g', 1, 'sf'): (-40.36, 1e9),
    ('gc',): (-24.56, None),
    ('gelu',): (-13.85, 2.5),
    ('gh', 0, 'relay'): (30.97, 3.0),
    ('gh', 0, 'spread'): (-14.58, 3.0),
    ('gh', 1, 'relay'): (-20.72, None),
    ('gh', 1, 'spread'): (17.11, 4.0),
    ('n', 'exchange'): (26.73, 4.0),
    ('n', 0, 'ff'): (16.27, 4.0),
    ('n', 0, 'firsts'): (-3.65, 1.0),
    ('n', 0, 's'): (-21.35, 0.5),
    ('n', 0, 'seconds'): (1.58, 3.0),
    ('n', 0, 'sf'): (15.74, None),
    ('n', 1, 'ff'): (-58.75, 2.0),
    ('n', 1, 'firsts'): (-1.73, 1.0),
    ('n', 1, 's'): (-16.0, 3.0),
    ('n', 1, 'seconds'): (0.81, 6.0),
    ('n', 1, 'sf'): (-18.02, None),
    ('own', 0): (-4.16, 1.5),
    ('own', 1): (33.36, 2.5),
    ('p1', 0): (-37.69, 4.0),
    ('p1', 1): (-22.43, None),
    ('partial', 0): (45.97, 6.0),
    ('partial', 1): (-1.22, 2.0),
    ('rs', 'end'): (39.5, 2.0),
    ('rs', 'yh'): (-20.47, 2.5),
    ('rs', 0, 's1'): (-22.5, None),
    ('rs', 0, 's2'): (-37.73, None),
    ('rs', 0, 's3'): (17.91, 6.0),
    ('rs', 0, 't2'): (-5.6, 2.5),
    ('rs', 1, 's1'): (-6.41, 4.0),
    ('rs', 1, 's2'): (-3.32, 0.5),
    ('rs', 1, 's3'): (-1.37, None),
    ('rs', 1, 't2'): (32.44, None),
    ('wi',): (25.65, 2.0),
    ('wo',): (1.57, 1.5),
    ('wp',): (38.35, 1.0),
}
LATENCY, STRETCH, PER_COPY = 2.235, 1.417, 0.03


def group(n):
    if n[0] in ("g", "n"):
        if len(n) <= 3:
            return n
        return (n[0], n[1], n[3] if n[3] in ("ff", "s") else n[4])
    if n[0] == "rs":
        return n[:2] if n[1] in ("yh", "end") else ("rs", n[1], n[3])
    if n[0] == "gh":
        return ("gh", n[1], n[3])
    if n[0] == "act":
        return ("act", n[2])
    if n[0] in ("partial", "p1", "own"):
        return n[:2]
    return n[:1] if n[0] in ("wo", "wp", "wi", "c1", "cown", "gelu") else n


def nt(left, right):
    return lax.dot_general(left, right, (((1,), (1,)), ((), ())), preferred_element_type=f32)


def nn(left, right):
    return lax.dot_general(left, right, (((1,), (0,)), ((), ())), preferred_element_type=f32)


def tn(left, right):
    return lax.dot_general(left, right, (((0,), (0,)), ((), ())), preferred_element_type=f32)


class Place:
    def __init__(self, block):
        gx, gy, gz = (lax.axis_index(a) for a in ("gx", "gy", "gz"))
        self.block = block
        self.z, self.yh, self.x, self.gz = gx // 2, lax.rem(gx, 2), gy, gz
        self.yl, self.c = gz // 2, lax.rem(gz, 2)
        z, yh, x = self.z, self.yh, self.x
        zp, zm, z2 = (lax.rem(z + k, 4) for k in (1, 3, 2))
        xp, xm, x2 = (lax.rem(x + k, 4) for k in (1, 3, 2))
        self.zs = (z, zp, zm, z2)
        self.xs = (x, xp, xm, x2)
        self.dev = {
            "x+": (gx, xp, gz),
            "x-": (gx, xm, gz),
            "z+": (zp * 2 + yh, x, gz),
            "z-": (zm * 2 + yh, x, gz),
            "yh": (z * 2 + 1 - yh, x, gz),
            "yl": (gx, gy, (1 - self.yl) * 2 + self.c),
            "c": (gx, gy, self.yl * 2 + 1 - self.c),
        }

    def rows(self, z, yh, x):
        return pl.ds(pl.multiple_of((z * 8 + yh * 4 + x) * self.block, self.block), self.block)

    def chunk(self, z, yh):
        n = 4 * self.block
        return pl.ds(pl.multiple_of((z * 2 + yh) * n, n), n)

    def shard(self, j):
        n = 8 * self.block
        return pl.ds(pl.multiple_of(j * n, n), n)


class Plan:
    rate = {"x+": 46e3, "x-": 46e3, "z+": 46e3, "z-": 46e3, "y": 46e3, "c": 6e5}
    latency = LATENCY

    def __init__(self, place, send_sems, recv_sems):
        self.place, self.ss, self.rs = place, send_sems, recv_sems
        self.tasks, self.index, self.recv, self.local = {}, {}, {}, {}
        self.done, self.copies = set(), {}

    def load(self, key, copy, at):
        copy.start()
        self.local[key] = (copy, at)

    def add(self, name, prio, fn=None, needs=(), after=(), sends=(), dur=0.1, backlog=1e9):
        shift, queue = TUNE.get(group(name), (0.0, None))
        prio, backlog = prio + shift, backlog if queue is None else queue
        self.tasks[name] = (prio, fn, tuple(needs), tuple(after), tuple(sends), dur, backlog)
        for key, src, dst, to, here in sends:
            self.index[key] = len(self.index)
            self.recv[key] = here

    def order(self):
        arrive = {k: at for k, (_, at) in self.local.items()}
        free = dict.fromkeys(self.rate, 0.0)
        left, finished, now, out = dict(self.tasks), set(), 0.0, []
        self.log = []
        while left:
            ready, times = [], []
            for name, (prio, fn, needs, after, sends, dur, backlog) in left.items():
                if any(a not in finished for a in after) or any(k not in arrive for k in needs):
                    continue
                at = max([arrive[k] for k in needs], default=0.0)
                for s in sends:
                    at = max(at, free[self.link(s[3])] - backlog)
                if at <= now:
                    ready.append((prio, len(ready), name))
                else:
                    times.append(at)
            if not ready:
                now = min(times)
                continue
            name = min(ready)[2]
            prio, fn, needs, after, sends, dur, backlog = left.pop(name)
            self.log.append((now, name))
            now += dur * STRETCH
            for key, src, dst, to, here in sends:
                link = self.link(to)
                size = math.prod(here.shape) * jnp.dtype(here.dtype).itemsize
                free[link] = max(free[link], now) + size / self.rate[link] + PER_COPY
                arrive[key] = free[link] + self.latency
            finished.add(name)
            out.append(name)
        self.log.append((max(now, max(free.values())), "end"))
        return out

    def link(self, to):
        return "y" if to in ("yl", "yh") else to

    def copy(self, key, src, dst, to):
        i = self.index[key]
        return pltpu.make_async_remote_copy(
            src_ref=src, dst_ref=dst, send_sem=self.ss.at[i], recv_sem=self.rs.at[i],
            device_id=self.place.dev[to], device_id_type=MESH)

    def wait(self, key):
        if key in self.done:
            return
        self.done.add(key)
        if key in self.local:
            self.local[key][0].wait()
        else:
            self.copy(key, self.recv[key], self.recv[key], "x+").wait_recv()

    def sent(self, keep):
        for key in [k for k in self.copies if keep(k)]:
            self.copies.pop(key).wait_send()

    def run(self):
        for name in self.order():
            prio, fn, needs, after, sends, dur, backlog = self.tasks[name]
            for k in needs:
                self.wait(k)
            if fn is not None:
                fn()
            for key, src, dst, to, here in sends:
                self.copies[key] = self.copy(key, src, dst, to)
                self.copies[key].start()
        for key in list(self.local) + list(self.index):
            self.wait(key)
        self.sent(lambda k: True)


WAYS = (("x+", "x-"), ("z+", "z-"))


def add_gather(plan, name, full, prio, backlogs, exchange):
    p = plan.place
    width = full.shape[1] // 2
    one, two = (p.xs, p.zs), (p.zs, p.xs)

    def view(part, yy, i, j, half=None):
        zz, xx = (j, i) if part == 0 else (i, j)
        start, n = part * width, width
        if half is not None:
            n = width // 2
            start += half * n
        return full.at[p.rows(zz, yy, xx), pl.ds(start, n)]

    own = full.at[p.rows(p.z, p.yh, p.x)]
    plan.add((name, "exchange"), exchange[0], needs=[("load", name)], after=exchange[1], backlog=exchange[2],
             sends=[((name, "y"), own, own, "yh", full.at[p.rows(p.z, 1 - p.yh, p.x)])])
    arrived = ([], [])
    for w, yy in ((0, p.yh), (1, 1 - p.yh)):
        pr = prio + w
        backlog = backlogs[w]
        start = [("load", name)] if w == 0 else [(name, "y")]
        got = arrived[w]

        def copy(key, v, to, here):
            return ((name, w) + key, v, v, to, here)

        firsts, seconds = [], []
        for q in (0, 1):
            i0, ip, im, i2 = one[q]
            j0, jp, jm, j2 = two[q]
            for s, near in ((0, im), (1, ip)):
                firsts.append(copy((q, "f", s), view(q, yy, i0, j0), WAYS[q][s], view(q, yy, near, j0)))
            for s, near in ((0, jm), (1, jp)):
                seconds.append(copy((q, 0, "s", s), view(q, yy, i0, j0), WAYS[1 - q][s], view(q, yy, i0, near)))
        plan.add((name, w, "firsts"), pr, needs=start, sends=firsts, backlog=backlog)
        plan.add((name, w, "seconds"), pr + 0.3, needs=start, sends=seconds, backlog=backlog)
        for q in (0, 1):
            i0, ip, im, i2 = one[q]
            j0, jp, jm, j2 = two[q]
            for s, i in ((0, im), (1, ip)):
                plan.add((name, w, q, "ff", s), pr, needs=[(name, w, q, "f", s)], backlog=backlog, sends=[
                    copy((q, "ff", s), view(q, yy, i, j0, s), WAYS[q][s], view(q, yy, i2, j0, s))])
            for k, i, needs in ((1, im, ["f0"]), (2, ip, ["f1"]), (3, i2, ["ff0", "ff1"])):
                plan.add((name, w, q, "s", k), pr + 0.2, needs=[(name, w, q, n[:-1], int(n[-1])) for n in needs],
                         backlog=backlog, sends=[
                    copy((q, k, "s", s), view(q, yy, i, j0), WAYS[1 - q][s], view(q, yy, i, near))
                    for s, near in ((0, jm), (1, jp))])
            for k, i in enumerate((i0, im, ip, i2)):
                for s, near in ((0, jm), (1, jp)):
                    plan.add((name, w, q, k, "sf", s), pr + 0.1, needs=[(name, w, q, k, "s", s)], backlog=backlog, sends=[
                        copy((q, k, "sf", s), view(q, yy, i, near, s), WAYS[1 - q][s], view(q, yy, i, j2, s))])
                    got += [(name, w, q, k, "s", s), (name, w, q, k, "sf", s)]
            got += [(name, w, q, "f", 0), (name, w, q, "f", 1), (name, w, q, "ff", 0), (name, w, q, "ff", 1)]
        got += start
    return arrived


def add_scatter(plan, d, far1, near1, far2, near2, keep, ys, yr, gn, prio, backlogs):
    p = plan.place
    width = d.shape[1] // 2
    one, two = (p.zs, p.xs), (p.xs, p.zs)

    def view(part, yy, i, j, half=None):
        zz, xx = (i, j) if part == 0 else (j, i)
        start, n = part * width, width
        if half is not None:
            n = width // 2
            start += half * n
        return d.at[p.rows(zz, yy, xx), pl.ds(start, n)]

    def fold(into, *terms):
        def fn():
            total = into[...].astype(f32)
            for t in terms:
                total = total + t[...].astype(f32)
            into[...] = total.astype(into.dtype)
        return fn

    for w, yy in ((0, 1 - p.yh), (1, p.yh)):
        pr = prio + w
        b = backlogs[w]
        for q in (0, 1):
            first, second = WAYS[1 - q], WAYS[q]
            j0, jp, jm, j2 = two[q]
            js = (j2, jp, jm, j0)
            slot = (3, 1, 2, 0)

            def part_of(i, k):
                return ("partial", w, i if q == 0 else slot[k])

            for k, j in enumerate(js):
                far = [("rs", w, q, "far1", k, h) for h in (0, 1)]
                near = [("rs", w, q, "near1", k, h) for h in (0, 1)]
                plan.add(("rs", w, q, "s1", k), pr + 0.1, after=[part_of(3, k)], backlog=b, sends=[
                    (far[h], view(q, yy, one[q][3], j, h), far1.at[w, q, k, h], first[h], far1.at[w, q, k, h])
                    for h in (0, 1)])
                for h in (0, 1):
                    i = 1 + h
                    plan.add(("rs", w, q, "s2", k, h), pr + 0.05 * k / 4, fold(view(q, yy, one[q][i], j, h), far1.at[w, q, k, h]),
                             needs=[far[h]], after=[part_of(i, k)], dur=0.15, backlog=b, sends=[
                        (near[h], view(q, yy, one[q][i], j), near1.at[w, q, k, h], first[h], near1.at[w, q, k, h])])
                mine = view(q, yy, one[q][0], j)
                if k < 3:
                    fn = fold(mine, near1.at[w, q, k, 0], near1.at[w, q, k, 1])
                else:
                    def fn(mine=mine, w=w, q=q, k=k):
                        keep[w, q] = (mine[...].astype(f32) + near1[w, q, k, 0].astype(f32)
                                      + near1[w, q, k, 1].astype(f32))
                plan.add(("rs", w, q, "s3", k), pr - 0.1, fn, needs=near, after=[part_of(0, k)], dur=0.25, sends=[
                    (("rs", w, q, "far2", h), view(q, yy, one[q][0], j, h), far2.at[w, q, h], second[h], far2.at[w, q, h])
                    for h in (0, 1)] if k == 0 else [])
            for h in (0, 1):
                plan.add(("rs", w, q, "t2", h), pr - 0.2, fold(view(q, yy, one[q][0], two[q][1 + h], h), far2.at[w, q, h]),
                         needs=[("rs", w, q, "far2", h)], after=[("rs", w, q, "s3", 1 + h)], dur=0.15, sends=[
                    (("rs", w, q, "near2", h), view(q, yy, one[q][0], two[q][1 + h]), near2.at[w, q, h], second[h],
                     near2.at[w, q, h])])
            cols = pl.ds(q * width, width)

            def total(w=w, q=q):
                return keep[w, q] + near2[w, q, 0].astype(f32) + near2[w, q, 1].astype(f32)

            needs = [("rs", w, q, "near2", h) for h in (0, 1)]
            if w == 0:
                def fn(total=total, cols=cols):
                    ys[:, cols] = total()
                plan.add(("rs", "yh", q), pr - 0.3, fn, needs=needs, after=[("rs", w, q, "s3", 3)], dur=0.2,
                         sends=[(("yh", q), ys.at[:, cols], yr.at[:, cols], "yh", yr.at[:, cols])])
            else:
                def fn(total=total, cols=cols):
                    gn[:, cols] = (total() + yr[:, cols]).astype(bf16)
                plan.add(("rs", "end", q), pr - 0.3, fn, needs=needs + [("yh", q)], after=[("rs", w, q, "s3", 3)], dur=0.2)


def kernel(scale, n_in, c_in, h_in, g_in, wi_in, wo_in, wp_in,
           gn_out, gc_out, gwi_out, gwo_out, gwp_out,
           G, N, ACT, CTX, HP, WIN, WOUT, WPROJ, GH, SLOPE, P1S, P1R, POWN, P2S, P2R,
           C1S, C1R, COWN, C2S, C2R, FAR1, NEAR1, FAR2, NEAR2, KEEP, YS, YR, ss, rs, ls):
    block = g_in.shape[0]
    p = Place(block)
    z, yh, x, gz, yl, c = p.z, p.yh, p.x, p.gz, p.yl, p.c
    o = 1 - yh
    n = 4 * block
    plan = Plan(p, ss, rs)
    other_y, other_c, other_yc = (1 - yl) * 2 + c, yl * 2 + 1 - c, (1 - yl) * 2 + 1 - c

    bar = pltpu.get_barrier_semaphore()
    for d in p.dev.values():
        pl.semaphore_signal(bar, inc=1, device_id=d, device_id_type=MESH)
    for i, (name, src, dst, at) in enumerate((
            ("g", g_in, G.at[p.rows(z, yh, x)], 0.0), ("h", h_in, HP, 0.0), ("c", c_in, CTX.at[gz], 0.0),
            ("n", n_in, N.at[p.rows(z, yh, x)], 0.0), ("wo", wo_in, WOUT, 1.0), ("wp", wp_in, WPROJ, 2.0),
            ("wi", wi_in, WIN, 3.0))):
        plan.load(("load", name), pltpu.make_async_copy(src, dst, ls.at[i]), at)
    plan.wait(("load", "h"))

    @pl.loop(0, HP.shape[0] // 16)
    def _(i):
        here = pl.ds(pl.multiple_of(i * 16, 16), 16)
        v = HP[here, :].astype(f32)
        cdf = 0.5 * (1.0 + lax.erf(v * inv_root_two))
        density = jnp.exp(-0.5 * v * v) * inv_root_two_pi
        SLOPE[here, :] = cdf + v * density
        ACT[pl.ds(pl.multiple_of(gz * HP.shape[0] + i * 16, 16), 16), :] = (v * cdf).astype(bf16)

    pl.semaphore_wait(bar, len(p.dev))

    g_got = add_gather(plan, "g", G, 0, K["g"], (-1, (), 0.5))
    n_got = add_gather(plan, "n", N, 20, K["n"], K["nx"])

    def spread(key, view, prio, needs=(), after=(), fn=None, dur=0.1, backlog=1e9, relay=None):
        plan.add(key + ("spread",), prio, fn, needs=needs, after=after, dur=dur, backlog=backlog, sends=[
            (key + ("y",), view(gz), view(gz), "yl", view(other_y)),
            (key + ("c",), view(gz), view(gz), "c", view(other_c))])
        plan.add(key + ("relay",), prio + 0.1 if relay is None else relay, needs=[key + ("y",)], sends=[
            (key + ("cy",), view(other_y), view(other_y), "c", view(other_yc))])
        return [key + (k,) for k in ("y", "c", "cy")]

    act_got = []
    pieces = K["pieces"]
    half_rows = HP.shape[0] // pieces
    for half in range(pieces):
        plan.add(("gelu", half), 1.5, needs=[("load", "h")], after=[("g", 0, "seconds")], dur=1.2 / pieces)
        act_got += spread(("act", half), lambda j, half=half: ACT.at[pl.ds(
            pl.multiple_of((j * pieces + half) * half_rows, half_rows), half_rows)], K["act"], after=[("gelu", half), ("g", "exchange")],
            backlog=K["ab"])
    ctx_got = spread(("ctx",), lambda j: CTX.at[j], K["ctx"], needs=[("load", "c")], after=[("g", "exchange")],
                     backlog=K["ab"])

    wave_yh = (yh, o)
    gh_got = ([], [])
    sub = n // 2
    for w in (0, 1):
        for s, yy in enumerate((1 - yl, yl)):
            def peer(w=w, s=s, yy=yy):
                P1S[w, s] = nt(G[p.chunk(yy * 2 + 1 - c, wave_yh[w]), :], WOUT[...])

            def own(w=w, s=s, yy=yy):
                v = nt(G[p.chunk(yy * 2 + c, wave_yh[w]), :], WOUT[...]) + P1R[w, s]
                if s == 0:
                    P2S[w] = v.astype(bf16)
                else:
                    POWN[w] = v

            plan.add(("p1", w, s), 3 + 0.1 * s, peer, needs=g_got[w] + [("load", "wo")], dur=0.95,
                     after=[("p1", w, 0)] if s else [], sends=[
                (("p1", w, s), P1S.at[w, s], P1R.at[w, s], "c", P1R.at[w, s])])
            plan.add(("own", w, s), 3.2 + 0.1 * s, own, needs=[("p1", w, s)], after=[("p1", w, 1)], dur=1.0, sends=[
                (("p2", w, h), P2S.at[w, pl.ds(h * sub, sub)], P2R.at[w, pl.ds(h * sub, sub)], "yl",
                 P2R.at[w, pl.ds(h * sub, sub)]) for h in (0, 1)] if s == 0 else [])
        for h in (0, 1):
            def hidden(w=w, h=h):
                here = pl.ds(h * sub, sub)
                local = pl.ds(pl.multiple_of(wave_yh[w] * n + h * sub, sub), sub)
                rows = pl.ds(pl.multiple_of((gz * 2 + wave_yh[w]) * n + h * sub, sub), sub)
                GH[rows, :] = ((POWN[w, here] + P2R[w, here].astype(f32)) * SLOPE[local, :]).astype(bf16)

            gh_got[w].extend(spread(("gh", w, h), lambda j, w=w, h=h: GH.at[pl.ds(
                pl.multiple_of((j * 2 + wave_yh[w]) * n + h * sub, sub), sub)], 2, fn=hidden, needs=[("p2", w, h)],
                after=[("own", w, 1)] + [("gelu", i) for i in range(pieces)], dur=0.3))

    g_all = g_got[0] + g_got[1]
    for s, yy in enumerate((1 - yl, yl)):
        def peer(s=s, yy=yy):
            C1S[s] = nt(WPROJ[...], G[p.shard(yy * 2 + 1 - c), :])

        def own(s=s, yy=yy):
            v = nt(WPROJ[...], G[p.shard(yy * 2 + c), :]) + C1R[s]
            if s == 0:
                C2S[...] = v.astype(bf16)
            else:
                COWN[...] = v

        plan.add(("c1", s), 30 + s, peer, needs=g_all + [("load", "wp")], dur=0.6,
                 after=[("c1", 0)] if s else [], sends=[
            (("c1", s), C1S.at[s], C1R.at[s], "c", C1R.at[s])])
        plan.add(("cown", s), 32 + s, own, needs=[("c1", s)], after=[("c1", 1)], dur=0.6)

    plan.add(("c2",), 60, needs=[], after=[("cown", 0), ("gh", 1, 0, "spread"), ("gh", 1, 1, "spread")],
             sends=[(("c2",), C2S, C2R, "yl", C2R)])

    def ctx_done():
        gc_out[...] = (COWN[...] + C2R[...].astype(f32)).astype(bf16)

    plan.add(("gc",), 70, ctx_done, needs=[("c2",)], after=[("cown", 1)], dur=0.1)

    readers = [("own", w, s) for w in (0, 1) for s in (0, 1)] + [("cown", 0), ("cown", 1)]
    for f in range(WOUT.shape[0] // 256):
        for t in range(3):
            def tile(f=f, t=t):
                rows, cols = pl.ds(f * 256, 256), pl.ds(t * 512, 512)
                gwo_out[rows, cols] = (tn(ACT[:, rows], G[:, cols]) * scale).astype(bf16)

            plan.add(("wo", f, t), 40, tile, needs=g_all + act_got, dur=0.75)
            readers.append(("wo", f, t))
    for t in range(3):
        def tile(t=t):
            cols = pl.ds(t * 512, 512)
            total = nn(CTX[0], G[p.shard(0), cols])
            for j in range(1, 4):
                total += nn(CTX[j], G[p.shard(j), cols])
            gwp_out[:, cols] = (total * scale).astype(bf16)

        plan.add(("wp", t), 46, tile, needs=g_all + ctx_got, dur=0.65)
    readers += [("wp", t) for t in range(3)]

    plan.add(("g", "sent"), 48, lambda: plan.sent(lambda k: k[0] == "g"), after=readers
             + [k for k in plan.tasks if k[0] == "g"], dur=0.1)
    for w, yy in ((0, o), (1, yh)):
        for i in (3, 1, 2, 0):
            def partial(i=i, yy=yy):
                rows = p.chunk(p.zs[i], yy)
                G[rows, :] = nt(GH[rows, :], WIN[...]).astype(bf16)

            plan.add(("partial", w, i), 4 + w * 8 + 0.01 * ((3, 1, 2, 0).index(i)), partial, needs=gh_got[1 - w] + [("load", "wi")],
                     after=[("g", "sent"), ("gh", 1 - w, 0, "spread"), ("gh", 1 - w, 1, "spread")], dur=1.0)
    add_scatter(plan, G, FAR1, NEAR1, FAR2, NEAR2, KEEP, YS, YR, gn_out, 7, K["rs"])

    parts = [("partial", w, i) for w in (0, 1) for i in range(4)]
    for t in range(N.shape[1] // 256):
        def tile(t=t):
            cols = pl.ds(t * 256, 256)
            gwi_out[cols, :] = (tn(N[:, cols], GH[...]) * scale).astype(bf16)

        plan.add(("wi", t), 80, tile, needs=n_got[0] + n_got[1], after=parts, dur=1.1)

    plan.run()


def copy_out(*refs):
    copies = [pltpu.make_async_copy(refs[i], refs[5 + i], refs[10].at[i]) for i in range(5)]
    for c in copies:
        c.start()
    for c in copies:
        c.wait()


def body(normed, context, hidden_pre, grad_out, w_in, w_out, w_proj):
    block, width = grad_out.shape
    shard, hidden = hidden_pre.shape
    feats = context.shape[1]
    tokens = 32 * block
    chunk = 4 * block
    half = width // 2
    scratch = [
        pltpu.VMEM((tokens, width), bf16),
        pltpu.VMEM((tokens, width), bf16),
        pltpu.VMEM((tokens, hidden), bf16),
        pltpu.VMEM((4, feats, shard), bf16),
        pltpu.VMEM((shard, hidden), bf16),
        pltpu.VMEM(w_in.shape, bf16),
        pltpu.VMEM(w_out.shape, bf16),
        pltpu.VMEM(w_proj.shape, bf16),
        pltpu.VMEM((tokens, hidden), bf16),
        pltpu.VMEM((shard, hidden), f32),
        pltpu.VMEM((2, 2, chunk, hidden), f32),
        pltpu.VMEM((2, 2, chunk, hidden), f32),
        pltpu.VMEM((2, chunk, hidden), f32),
        pltpu.VMEM((2, chunk, hidden), bf16),
        pltpu.VMEM((2, chunk, hidden), bf16),
        pltpu.VMEM((2, feats, shard), f32),
        pltpu.VMEM((2, feats, shard), f32),
        pltpu.VMEM((feats, shard), f32),
        pltpu.VMEM((feats, shard), bf16),
        pltpu.VMEM((feats, shard), bf16),
        pltpu.VMEM((2, 2, 4, 2, block, half // 2), bf16),
        pltpu.VMEM((2, 2, 4, 2, block, half), bf16),
        pltpu.VMEM((2, 2, 2, block, half // 2), bf16),
        pltpu.VMEM((2, 2, 2, block, half), bf16),
        pltpu.VMEM((2, 2, block, half), f32),
        pltpu.VMEM((block, width), f32),
        pltpu.VMEM((block, width), f32),
        pltpu.SemaphoreType.DMA((SEMS,)),
        pltpu.SemaphoreType.DMA((SEMS,)),
        pltpu.SemaphoreType.DMA((8,)),
    ]
    context = context.T
    outs = [normed, context, w_in, w_out, w_proj]

    def call(*refs):
        kernel(1.0 / math.sqrt(tokens), *refs)

    results = pl.pallas_call(
        call,
        out_shape=[pltpu.VMEM(v.shape, v.dtype) for v in outs],
        in_specs=[pl.BlockSpec(memory_space=pl.ANY)] * 7,
        out_specs=[pl.BlockSpec(memory_space=pltpu.VMEM)] * 5,
        scratch_shapes=scratch,
        compiler_params=pltpu.CompilerParams(
            collective_id=0, has_side_effects=True, vmem_limit_bytes=56 * 2**20),
    )(normed, context, hidden_pre, grad_out, w_in, w_out, w_proj)
    gn, gc, gwi, gwo, gwp = pl.pallas_call(
        copy_out,
        out_shape=[jax.ShapeDtypeStruct(v.shape, v.dtype) for v in outs],
        in_specs=[pl.BlockSpec(memory_space=pltpu.VMEM)] * 5,
        out_specs=[pl.BlockSpec(memory_space=pl.ANY)] * 5,
        scratch_shapes=[pltpu.SemaphoreType.DMA((5,))],
        compiler_params=pltpu.CompilerParams(vmem_limit_bytes=2**20),
    )(*results)
    return gn, gc.T, gwi, gwo, gwp


def solution(mesh):
    in_specs = (
        P(("gx", "gy"), "gz"),
        P("gz", ("gx", "gy")),
        P("gz", ("gx", "gy")),
        P(("gx", "gy"), "gz"),
        P("gz", ("gx", "gy")),
        P(("gx", "gy"), "gz"),
        P(("gx", "gy"), "gz"),
    )
    out_specs = (
        P(("gx", "gy"), "gz"),
        P("gz", ("gx", "gy")),
        P("gz", ("gx", "gy")),
        P(("gx", "gy"), "gz"),
        P(("gx", "gy"), "gz"),
    )
    return jax.shard_map(body, mesh=mesh, in_specs=in_specs, out_specs=out_specs, check_vma=False)
```
